128 devices in a mesh: rows: 16 (over z, y), serve: 8 (over x, core).
Axes of the slice: x: 4, y: 4, z: 4, core: 2. Of those that a mesh axis runs over, the one named last changes fastest.
Arguments:
- rows_small: float32 [131072, 32], P(('rows', 'serve')), may hold values from -6 to 6
- rows_mid: float32 [131072, 64], P(('rows', 'serve')), may hold values from -6 to 6
- rows_wide: float32 [131072, 128], P(('rows', 'serve')), may hold values from -6 to 6
- row_grads: float32 [3, 131072, 256], P(None, ('rows', 'serve'))
- proj_small: float32 [32, 256], replicated, may hold values from -1 to 1
- proj_mid: float32 [64, 256], replicated, may hold values from -0.75 to 0.75
- proj_wide: float32 [128, 256], replicated, may hold values from -0.5 to 0.5
- counts: int32 [3, 128], P(None, ('rows', 'serve')), may hold values from 512 to 1024, as said below
- owners: int32 [3, 131072, 1], P(None, ('rows', 'serve')), may hold values from 0 to 127; in each aligned block of 1024 rows (0 to 1023, 1024 to 2047, ..., all dimensions but the last counted through in order) at most 12 rows name the same one
Outputs:
- served: bfloat16 [196608, 768], P(('rows', 'serve'))
The draws below stay inside these ranges and needn't reach their ends.
Inputs may be any that keep to these rules, and one draw needn't show every extreme that they name: `counts`: one device of each tier has all 1024 slots live. `owners`: among the 1024 slots of one device and tier at most 12 name one owner, and exactly 12 do for some owner.
All inputs are finite; a program needn't handle non-finite values.
Results may differ from the reference program's by a relative error of at most 0.001.
Values may be sent and summed in bfloat16 or wider, within the bound.
A program may use at most 64 MiB of HBM per device.

```python
import math
import jax
import jax.numpy as jnp
import numpy as np
from jax import lax

W_SMALL = 32
W_MID = 64
W_WIDE = 128
D_OUT = 256
ROWS_DEV = 1024
ALL_DEVS = 128
TOTAL_ROWS = 131072
CAP = 12
N_ROWS = 16
N_SERVE = 8


def draw_row_grads(key, part):
    key = jax.random.fold_in(key, 11)
    first_key = jax.random.fold_in(key, 0)
    device_of = (jnp.arange(TOTAL_ROWS) // ROWS_DEV).astype(jnp.float32)
    rising = 1.0 + 2.0 * device_of / max(ALL_DEVS - 1, 1)
    values = jax.random.normal(first_key, (3, TOTAL_ROWS, D_OUT)) * rising[None, :, None]
    return values.astype(jnp.float32)


def draw_counts(key, part):
    key = jax.random.fold_in(key, 5)
    first_key, second_key = jax.random.split(key, 2)
    cuts = jax.random.randint(first_key, (3, ALL_DEVS), 0, ROWS_DEV // 256 + 1)
    chosen = jax.random.randint(second_key, (3, 1), 0, ALL_DEVS)
    cuts = jnp.where(jnp.arange(ALL_DEVS)[None, :] == chosen, 0, cuts)
    return (ROWS_DEV - 128 * cuts).astype(jnp.int32)


def steps_of(own_key, extent, cuts, low, high):
    factor_of = 1.0
    for dim, parts in cuts:
        draws = jax.random.uniform(jax.random.fold_in(jax.random.fold_in(own_key, 6), dim), (parts,), jnp.float32, low / len(cuts), high / len(cuts))
        factor_of = factor_of * jnp.repeat(jnp.exp(draws), extent[dim] // parts).reshape((-1,) + (1,) * (len(extent) - 1 - dim))
    return factor_of


def deal_out(key, own, number, rows, number_of, top, bound, lean):
    order = jax.random.permutation(key, number_of)
    crowded, usual = portions_of(number_of, rows * top, bound, lean, True), portions_of(number_of, rows * top, bound, lean, False)
    places = jnp.arange(number_of)

    def named(sizes, rotation):
        used = int((sizes > 0).sum())
        fixed = max(1, used // 4)
        moved = fixed + (places - fixed + rotation * (used - fixed)) % max(1, number_of - fixed)
        return jnp.zeros((number_of,), jnp.int32).at[order[jnp.where(places < fixed, places, moved)]].set(jnp.asarray(sizes, jnp.int32))

    sizes = jnp.where(number % 4 == 0, named(crowded, number // 4), named(usual, number - number // 4 - 1))
    mixed = jax.random.permutation(jax.random.fold_in(own, 3), number_of)
    donor, receiver = mixed[0:number_of // 2 * 2:2], mixed[1:number_of // 2 * 2:2]
    margin = jnp.minimum(sizes[donor] - 1, bound - sizes[receiver]) // 2
    margin = jnp.where((donor == order[0]) | (receiver == order[0]) | (sizes[receiver] == 0), 0, jnp.maximum(margin, 0))
    moved = jax.random.randint(jax.random.fold_in(own, 4), (number_of // 2,), 0, 1 << 20) % (margin + 1)
    sizes = sizes.at[donor].add(-moved).at[receiver].add(moved)
    members = jnp.searchsorted(jnp.cumsum(sizes), jnp.arange(rows * top), side="right").astype(jnp.int32)
    table = members.reshape(top, rows).T
    table = table[jax.random.permutation(jax.random.fold_in(own, 1), rows)]
    rotation = jax.random.randint(jax.random.fold_in(own, 2), (rows, 1), 0, top)
    return jnp.take_along_axis(table, (jnp.arange(top)[None, :] + rotation) % top, axis=1)


def portions_of(count, total, limit, lean, full):
    loads = [(1 << 20) // math.isqrt(rank ** lean) + 1 for rank in range(1, count + 1)]
    largest = limit if full else min(limit, max(-(-total // count), total * loads[0] // sum(loads)))
    least = 1 if total - largest >= count - 1 else 0
    holding, spare = [largest] + [least] * (count - 1), total - largest - least * (count - 1)
    while spare > 0:
        free = [i for i in range(1, count) if holding[i] < largest] or [i for i in range(1, count) if holding[i] < limit]
        whole, budget = sum([loads[i] for i in free]), spare
        for i in free:
            more = min(limit - holding[i], max(1, budget * loads[i] // whole), spare)
            holding[i] = holding[i] + more
            spare = spare - more
    return np.array(holding)


def gaussian(own_key, shape, width, reach, cuts=(), held_as=jnp.bfloat16):
    level = steps_of(own_key, shape, cuts, -0.22, 0.18) if cuts else 1.0
    array = jax.random.normal(own_key, shape, jnp.float32) * width * level
    return jnp.minimum(jnp.maximum(array, -reach), reach).astype(held_as)


def setup_inputs(seed: int = 0) -> dict:
    keys = jax.random.split(jax.random.key(seed), 10)
    rows_small = gaussian(keys[0], (TOTAL_ROWS, W_SMALL), 1.0, 6.0, ((0, 128),), jnp.float32)
    rows_mid = gaussian(keys[1], (TOTAL_ROWS, W_MID), 1.0, 6.0, ((0, 128),), jnp.float32)
    rows_wide = gaussian(keys[2], (TOTAL_ROWS, W_WIDE), 1.0, 6.0, ((0, 128),), jnp.float32)
    row_grads = draw_row_grads(jax.random.fold_in(keys[9], 71), 0)
    proj_small = gaussian(keys[4], (W_SMALL, D_OUT), W_SMALL ** -0.5, 1.0, (), jnp.float32)
    proj_mid = gaussian(keys[5], (W_MID, D_OUT), W_MID ** -0.5, 0.75, (), jnp.float32)
    proj_wide = gaussian(keys[6], (W_WIDE, D_OUT), W_WIDE ** -0.5, 0.5, (), jnp.float32)
    counts = draw_counts(jax.random.fold_in(keys[9], 71), 0)
    owners_keys = jax.random.split(jax.random.fold_in(keys[8], 1), 3 * TOTAL_ROWS // ROWS_DEV)
    owners_turns = jax.random.permutation(jax.random.fold_in(keys[8], 3), 3 * TOTAL_ROWS // ROWS_DEV)
    owners = jax.vmap(lambda own, number: deal_out(jax.random.fold_in(keys[8], 2), own, number, ROWS_DEV, ALL_DEVS, 1, CAP, 2))(owners_keys, owners_turns).reshape((3, TOTAL_ROWS, 1))
    return dict(rows_small=rows_small, rows_mid=rows_mid, rows_wide=rows_wide, row_grads=row_grads, proj_small=proj_small, proj_mid=proj_mid, proj_wide=proj_wide, counts=counts, owners=owners)


STEP_NORM = 16.0
ROW_RATE = 0.1

def refresh(projection, total):
    factor = STEP_NORM / jnp.sqrt(jnp.sum(total * total) + 1e-06)
    return projection - factor * total

def reference(rows_small, rows_mid, rows_wide, row_grads, proj_small, proj_mid, proj_wide, counts, owners):
    device_count = N_ROWS * N_SERVE
    capacity = CAP
    tables = (rows_small, rows_mid, rows_wide)
    projections = (proj_small, proj_mid, proj_wide)
    positions = jnp.arange(ROWS_DEV, dtype=jnp.int32)
    sources = jnp.arange(TOTAL_ROWS, dtype=jnp.int32) // ROWS_DEV
    columns = jnp.arange(device_count, dtype=jnp.int32)
    outside = device_count * device_count * capacity
    served = jnp.zeros((outside, 3 * D_OUT), jnp.bfloat16)
    for tier_index in range(3):
        table = tables[tier_index]
        projection = projections[tier_index]
        valid = (positions[None, :] < counts[tier_index][:, None]).reshape(-1)
        gradients = jnp.where(valid[:, None], row_grads[tier_index], 0.0)
        total = jnp.dot(table.T, gradients, precision=lax.Precision.HIGHEST, preferred_element_type=jnp.float32)
        new_proj = refresh(projection, total)
        row_step = jnp.dot(gradients, projection.T, precision=lax.Precision.HIGHEST, preferred_element_type=jnp.float32)
        new_rows = table - ROW_RATE * row_step
        projected = jnp.dot(new_rows, new_proj, precision=lax.Precision.HIGHEST, preferred_element_type=jnp.float32).astype(jnp.bfloat16)
        owner = owners[tier_index, :, 0]
        matched = (owner[:, None] == columns[None, :]) & valid[:, None]
        hit_counts = matched.astype(jnp.int32).reshape(device_count, ROWS_DEV, device_count)
        before = (jnp.cumsum(hit_counts, axis=1) - hit_counts).reshape(TOTAL_ROWS, device_count)
        slot_index = lax.optimization_barrier(jnp.sum(jnp.where(matched, before, 0), axis=1)).astype(jnp.int32)
        target = owner * (device_count * capacity) + sources * capacity + slot_index
        target = jnp.where(valid, target, outside).astype(jnp.int32)
        served = served.at[target, tier_index * D_OUT:(tier_index + 1) * D_OUT].set(projected, mode='drop')
    return served
```

```python
import functools

import jax
import jax.numpy as jnp
from jax import lax
from jax.experimental import pallas as pl
from jax.experimental.pallas import tpu as pltpu
from jax.sharding import PartitionSpec as P

STEP_NORM = 16.0
ROW_RATE = 0.1
MESH = pl.DeviceIdType.MESH
N_ROWS = 16
N_SERVE = 8
DEVS = 128
CAP = 12
SLOTS = DEVS * CAP
ROWS = 1024
D = 256
LANES = 128
BLOCK = 2 * CAP
PAIRS_STEP = 8
CHUNK = PAIRS_STEP * BLOCK
F32 = jnp.float32
BF16 = jnp.bfloat16


def split(x):
    high = x.astype(BF16)
    low = (x - high.astype(F32)).astype(BF16)
    return high, low


def dot(a, b):
    return lax.dot_general(a, b, (((1,), (0,)), ((), ())), preferred_element_type=F32)


def dot_nt(a, b):
    return lax.dot_general(a, b, (((1,), (1,)), ((), ())), preferred_element_type=F32)


def place_of(p):
    return (p // N_SERVE, p % N_SERVE)


def peer_of(me, r):
    z = (me // 32 + r // 32) % 4
    y = (me // 8 + r // 8) % 4
    x = (me // 2 + r // 2) % 4
    return z * 32 + y * 8 + x * 2 + (me + r) % 2


def half_turn(x):
    return pltpu.roll(x, 4, 1)


def front_kernel(
    small_hbm, mid_hbm, wide_hbm, grads_hbm, ps_hbm, pm_hbm, pw_hbm, counts_ref, owners_hbm,
    recv_hbm, weights_ref,
    small, mid, wide, grads, ps, pm, pw, owners,
    placed_w, placed_m, placed_s, targets, send, totals, stage1, sum1, stage2, full,
    in_sem, send_sem, recv_sem, red_send, red_recv, own_sem,
):
    rows_at = lax.axis_index("rows")
    serve_at = lax.axis_index("serve")
    me = rows_at * N_SERVE + serve_at

    sources = (owners_hbm, small_hbm, mid_hbm, wide_hbm, ps_hbm, pm_hbm, pw_hbm)
    holders = (owners, small, mid, wide, ps, pm, pw)
    loads = [pltpu.make_async_copy(s, h, in_sem.at[i]) for i, (s, h) in enumerate(zip(sources, holders))]
    grad_loads = [
        pltpu.make_async_copy(grads_hbm.at[t], grads.at[t], in_sem.at[len(loads) + t]) for t in range(3)
    ]
    for load in loads:
        load.start()
    for t in (2, 1, 0):
        grad_loads[t].start()

    barrier = pltpu.get_barrier_semaphore()

    def greet(j, carry):
        pl.semaphore_signal(barrier, inc=1, device_id=place_of(peer_of(me, j)), device_id_type=MESH)
        return carry

    lax.fori_loop(1, DEVS, greet, 0)

    loads[0].wait()
    lane = lax.broadcasted_iota(jnp.int32, (1, ROWS), 1)
    named = lax.broadcasted_iota(jnp.int32, (DEVS, ROWS), 0)
    hits = []
    for t in range(3):
        live = lane < counts_ref[0, t]
        owner = jnp.where(live, owners[t], -1)
        hits.append(jnp.where(named == owner, 1.0, 0.0).astype(BF16))
    hit = jnp.concatenate(hits, axis=0)
    ahead = lax.broadcasted_iota(jnp.int32, (256, 256), 0) < lax.broadcasted_iota(jnp.int32, (256, 256), 1)
    ahead = jnp.where(ahead, 1.0, 0.0).astype(BF16)
    carry = jnp.zeros((3 * DEVS, 1), F32)
    ranks = []
    for c in range(ROWS // 256):
        part = hit[:, c * 256:(c + 1) * 256]
        before = dot(part, ahead) + carry
        mine = part.astype(F32)
        carry = before[:, 255:256] + mine[:, 255:256]
        ranks.append(jnp.sum((before * mine).reshape(3, DEVS, 256), axis=1))
    rank = jnp.concatenate(ranks, axis=1).astype(jnp.int32)
    for t in range(3):
        owner = owners[t]
        turn = jnp.where(owner % 2 == me % 2, 0, jnp.where(owner % 2 == 0, 8, 4))
        slot = rank[t:t + 1] + turn
        slot = jnp.where(slot >= CAP, slot - CAP, slot)
        live = lane < counts_ref[0, t]
        targets[t] = jnp.where(live, owner * CAP + slot, -1)

    for load in loads[1:]:
        load.wait()
    wide_t = wide[...].T
    both_t = jnp.concatenate([mid[...], small[...], jnp.zeros((32, ROWS), F32)], axis=0)
    both = both_t.T
    column = lax.broadcasted_iota(jnp.int32, (ROWS, LANES), 1)
    zeros = lambda n: jnp.zeros((n, D), F32)
    tiers = (
        (2, wide_t, wide[...], pw[...], placed_w),
        (1, mid[...], jnp.where(column < 64, both, 0.0),
         jnp.concatenate([pm[...], zeros(64)], axis=0), placed_m),
        (0, small[...], jnp.where(column >= 64, both, 0.0),
         jnp.concatenate([zeros(64), ps[...], zeros(32)], axis=0), placed_s),
    )
    at = 0
    row = lax.broadcasted_iota(jnp.int32, (ROWS, D), 0)
    for t, table_t, table, projection, placed in tiers:
        grad_loads[t].wait()
        masked = jnp.where(row < counts_ref[0, t], grads[t], 0.0)
        g_high, g_low = split(masked)
        e_high, e_low = split(table_t)
        total = dot(e_high, g_high) + (dot(e_low, g_high) + dot(e_high, g_low))
        width = table_t.shape[0]
        totals[at:at + width, :] = total[:, :LANES]
        totals[at + width:at + 2 * width, :] = total[:, LANES:]
        at += 2 * width
        p_high, p_low = split(projection)
        step = dot_nt(g_high, p_high) + (dot_nt(g_low, p_high) + dot_nt(g_high, p_low))
        moved = table - ROW_RATE * step
        high, low = split(moved)
        placed[:, :LANES] = high
        placed[:, LANES:] = low
    totals[at:, :] = jnp.zeros((512 - at, LANES), F32)

    slot_row = lax.broadcasted_iota(jnp.int32, (CHUNK, ROWS), 0)
    lower = lax.broadcasted_iota(jnp.int32, (PAIRS_STEP, 8, LANES), 1) < 4

    def place(c, carry):
        base = c * CHUNK

        def chosen(t):
            return jnp.where(slot_row == targets[t] - base, 1.0, 0.0).astype(BF16)

        got_a = dot(chosen(2), placed_w[...])
        got_b = dot(chosen(1), placed_m[...]) + dot(chosen(0), placed_s[...])
        a = (got_a[:, :LANES] + got_a[:, LANES:]).reshape(PAIRS_STEP, BLOCK, LANES)
        b = (got_b[:, :LANES] + got_b[:, LANES:]).reshape(PAIRS_STEP, BLOCK, LANES)
        at = pl.ds(c * PAIRS_STEP, PAIRS_STEP)
        a_half, b_half = a[:, 8:16], b[:, 8:16]
        send[at, 0, 0:8] = a[:, 0:8]
        send[at, 0, 8:16] = b[:, 0:8]
        send[at, 0, 16:24] = jnp.where(lower, a_half, half_turn(b_half))
        send[at, 1, 0:8] = a[:, 16:24]
        send[at, 1, 8:16] = b[:, 16:24]
        send[at, 1, 16:24] = jnp.where(lower, half_turn(a_half), b_half)
        return carry

    lax.fori_loop(0, SLOTS // CHUNK, place, 0)

    pl.semaphore_wait(barrier, DEVS - 1)

    def route(j, carry):
        p = peer_of(me, (j * 37) % DEVS)
        pltpu.make_async_remote_copy(
            send.at[p // 2, p % 2], recv_hbm.at[me], send_sem, recv_sem,
            device_id=place_of(p), device_id_type=MESH,
        ).start()
        return carry

    def scatter_rows(j, carry):
        p = (rows_at + j) % N_ROWS
        pltpu.make_async_remote_copy(
            totals.at[pl.ds(pl.multiple_of(p * 32, 32), 32)], stage1.at[rows_at], red_send.at[0], red_recv.at[0],
            device_id=(p, serve_at), device_id_type=MESH,
        ).start()
        return carry

    def swap_serve(j, carry):
        p = (serve_at + j) % N_SERVE
        pltpu.make_async_remote_copy(
            sum1, stage2.at[serve_at], red_send.at[1], red_recv.at[1],
            device_id=(rows_at, p), device_id_type=MESH,
        ).start()
        return carry

    def gather_rows(j, carry):
        p = (rows_at + j) % N_ROWS
        pltpu.make_async_remote_copy(
            full.at[rows_at], full.at[rows_at], red_send.at[2], red_recv.at[2],
            device_id=(p, serve_at), device_id_type=MESH,
        ).start()
        return carry

    def all_of(ref, n, sem):
        pltpu.make_async_copy(ref.at[pl.ds(0, n)], ref.at[pl.ds(0, n)], sem).wait()

    lax.fori_loop(1, N_ROWS, scatter_rows, 0)
    own = pltpu.make_async_copy(send.at[me // 2, me % 2], recv_hbm.at[me], own_sem)
    own.start()
    lax.fori_loop(1, 48, route, 0)
    stage1[rows_at] = totals[pl.ds(pl.multiple_of(rows_at * 32, 32), 32), :]
    all_of(stage1, N_ROWS - 1, red_recv.at[0])
    sum1[...] = jnp.sum(stage1[...], axis=0)
    lax.fori_loop(1, N_SERVE, swap_serve, 0)
    lax.fori_loop(48, 88, route, 0)
    stage2[serve_at] = sum1[...]
    all_of(stage2, N_SERVE - 1, red_recv.at[1])
    full[rows_at] = jnp.sum(stage2[...], axis=0)
    lax.fori_loop(1, N_ROWS, gather_rows, 0)
    lax.fori_loop(88, DEVS, route, 0)
    all_of(full, N_ROWS - 1, red_recv.at[2])

    summed = full[...].reshape(512, LANES)
    at = 0
    fresh = []
    for projection in (pw[...], pm[...], ps[...]):
        width = projection.shape[0]
        total = jnp.concatenate([summed[at:at + width], summed[at + width:at + 2 * width]], axis=1)
        at += 2 * width
        size = jnp.sum(total * total, axis=(0, 1), keepdims=True)
        fresh.append(projection - (STEP_NORM / jnp.sqrt(size + 1e-06)) * total)
    columns = (
        jnp.concatenate([zeros(64), fresh[2], zeros(32)], axis=0),
        jnp.concatenate([fresh[1], zeros(64)], axis=0),
        fresh[0],
    )
    for t in range(3):
        high, low = split(columns[t])
        weights_ref[0:128, t * D:(t + 1) * D] = high
        weights_ref[128:256, t * D:(t + 1) * D] = high
        weights_ref[256:384, t * D:(t + 1) * D] = low

    own.wait()
    all_of(recv_hbm, DEVS - 1, recv_sem)
    pltpu.make_async_copy(recv_hbm.at[pl.ds(0, DEVS - 1)], recv_hbm.at[pl.ds(0, DEVS - 1)], send_sem).wait()
    all_of(stage1, N_ROWS - 1, red_send.at[0])
    all_of(stage2, N_SERVE - 1, red_send.at[1])
    all_of(full, N_ROWS - 1, red_send.at[2])


def project_kernel(recv_ref, weights_ref, out_ref):
    pairs = recv_ref.shape[0] // 2
    got = recv_ref[...].reshape(pairs, 2, BLOCK, LANES)
    even, odd = got[:, 0], got[:, 1]
    lower = lax.broadcasted_iota(jnp.int32, (pairs, 8, LANES), 1) < 4
    even_half, odd_half = even[:, 16:24], odd[:, 16:24]
    a_half = jnp.where(lower, even_half, half_turn(odd_half))
    b_half = jnp.where(lower, half_turn(even_half), odd_half)
    a = jnp.concatenate([even[:, 0:8], a_half, odd[:, 0:8]], axis=1).reshape(pairs * BLOCK, LANES)
    b = jnp.concatenate([even[:, 8:16], b_half, odd[:, 8:16]], axis=1).reshape(pairs * BLOCK, LANES)
    for rows, first, last in ((b, 0, 2 * D), (a, 2 * D, 3 * D)):
        high, low = split(rows)
        both = jnp.concatenate([high, low, high], axis=1)
        out_ref[:, first:last] = dot(both, weights_ref[:, first:last]).astype(BF16)


def local(rows_small, rows_mid, rows_wide, row_grads, proj_small, proj_mid, proj_wide, counts, owners):
    hbm = pl.BlockSpec(memory_space=pl.ANY)
    vmem = pl.BlockSpec(memory_space=pltpu.VMEM)
    recv, weights = pl.pallas_call(
        front_kernel,
        out_shape=(
            jax.ShapeDtypeStruct((DEVS, BLOCK, LANES), F32),
            jax.ShapeDtypeStruct((384, 3 * D), BF16),
        ),
        in_specs=[hbm] * 7 + [pl.BlockSpec(memory_space=pltpu.SMEM), hbm],
        out_specs=(hbm, vmem),
        scratch_shapes=[
            pltpu.VMEM((32, ROWS), F32),
            pltpu.VMEM((64, ROWS), F32),
            pltpu.VMEM((ROWS, LANES), F32),
            pltpu.VMEM((3, ROWS, D), F32),
            pltpu.VMEM((32, D), F32),
            pltpu.VMEM((64, D), F32),
            pltpu.VMEM((128, D), F32),
            pltpu.VMEM((3, 1, ROWS), jnp.int32),
            pltpu.VMEM((ROWS, 2 * LANES), BF16),
            pltpu.VMEM((ROWS, 2 * LANES), BF16),
            pltpu.VMEM((ROWS, 2 * LANES), BF16),
            pltpu.VMEM((3, 1, ROWS), jnp.int32),
            pltpu.VMEM((DEVS // 2, 2, BLOCK, LANES), F32),
            pltpu.VMEM((512, LANES), F32),
            pltpu.VMEM((N_ROWS, 32, LANES), F32),
            pltpu.VMEM((32, LANES), F32),
            pltpu.VMEM((N_SERVE, 32, LANES), F32),
            pltpu.VMEM((N_ROWS, 32, LANES), F32),
            pltpu.SemaphoreType.DMA((10,)),
            pltpu.SemaphoreType.DMA,
            pltpu.SemaphoreType.DMA,
            pltpu.SemaphoreType.DMA((3,)),
            pltpu.SemaphoreType.DMA((3,)),
            pltpu.SemaphoreType.DMA,
        ],
        compiler_params=pltpu.CompilerParams(
            collective_id=0, has_side_effects=True, vmem_limit_bytes=48 << 20
        ),
        cost_estimate=pl.CostEstimate(flops=4_000_000_000, bytes_accessed=8_000_000, transcendentals=0),
        name="step_and_route",
    )(
        rows_small.T, rows_mid.T, rows_wide, row_grads, proj_small, proj_mid, proj_wide,
        counts.T, jnp.transpose(owners, (0, 2, 1)),
    )
    step = 16
    return pl.pallas_call(
        project_kernel,
        grid=(DEVS // step,),
        out_shape=jax.ShapeDtypeStruct((SLOTS, 3 * D), BF16),
        in_specs=[
            pl.BlockSpec((step, BLOCK, LANES), lambda i: (i, 0, 0)),
            pl.BlockSpec((384, 3 * D), lambda i: (0, 0)),
        ],
        out_specs=pl.BlockSpec((step * CAP, 3 * D), lambda i: (i, 0)),
        compiler_params=pltpu.CompilerParams(vmem_limit_bytes=32 << 20),
        cost_estimate=pl.CostEstimate(flops=1_000_000_000, bytes_accessed=5_000_000, transcendentals=0),
        name="project",
    )(recv, weights)


def solution(mesh):
    return jax.shard_map(
        local,
        mesh=mesh,
        in_specs=(
            P(("rows", "serve"), None),
            P(("rows", "serve"), None),
            P(("rows", "serve"), None),
            P(None, ("rows", "serve"), None),
            P(),
            P(),
            P(),
            P(None, ("rows", "serve")),
            P(None, ("rows", "serve"), None),
        ),
        out_specs=P(("rows", "serve"), None),
        check_vma=False,
    )
```

```python
import functools

import jax
import jax.numpy as jnp
from jax import lax
from jax.experimental import pallas as pl
from jax.experimental.pallas import tpu as pltpu
from jax.sharding import PartitionSpec as P

STEP_NORM = 16.0
ROW_RATE = 0.1
MESH = pl.DeviceIdType.MESH
N_ROWS = 16
N_SERVE = 8
DEVS = 128
CAP = 12
SLOTS = DEVS * CAP
ROWS = 1024
D = 256
LANES = 128
GROUP = 16
CHUNK = GROUP * CAP
CHUNKS = DEVS // GROUP
SHARE = 7
FINE = 64
F32 = jnp.float32
BF16 = jnp.bfloat16


def split(x):
    high = x.astype(BF16)
    low = (x - high.astype(F32)).astype(BF16)
    return high, low


def dot(a, b):
    return lax.dot_general(a, b, (((1,), (0,)), ((), ())), preferred_element_type=F32)


def dot_nt(a, b):
    return lax.dot_general(a, b, (((1,), (1,)), ((), ())), preferred_element_type=F32)


def scale_code(size):
    code = jnp.ceil(jnp.log2(jnp.maximum(size, 2.0 ** -109)) * FINE)
    return jnp.minimum(jnp.maximum(code, -110.0 * FINE), 128.0 * FINE)


def scale_up(code):
    return jnp.exp2(15.0 - code * (1.0 / FINE))


def fixed(x, factor):
    return jnp.clip(jnp.floor(x * factor + 0.5), -32767.0, 32767.0)


def front_kernel(
    small_hbm, mid_hbm, wide_hbm, grads_hbm, ps_hbm, pm_hbm, pw_hbm, counts_ref, owners_hbm,
    recv_hbm, weights_ref,
    small, mid, wide, grads, ps, pm, pw, owners,
    placed_w, placed_m, placed_s, targets, send, totals, stage1, sum1, stage2, full,
    in_sem, send_sem, recv_sem, red_send, red_recv, own_sem,
):
    rows_at = lax.axis_index("rows")
    serve_at = lax.axis_index("serve")
    me = rows_at * N_SERVE + serve_at
    z, y, x, core = rows_at // 4, rows_at % 4, serve_at // 2, serve_at % 2
    zs = [(z + d) % 4 * 4 for d in range(4)]
    ys = [(y + d) % 4 for d in range(4)]
    xs = [(x + d) % 4 * 2 for d in range(4)]
    cores = [core, 1 - core]

    sources = (owners_hbm, small_hbm, mid_hbm, wide_hbm, ps_hbm, pm_hbm, pw_hbm)
    holders = (owners, small, mid, wide, ps, pm, pw)
    loads = [pltpu.make_async_copy(s, h, in_sem.at[i]) for i, (s, h) in enumerate(zip(sources, holders))]
    grad_loads = [
        pltpu.make_async_copy(grads_hbm.at[t], grads.at[t], in_sem.at[len(loads) + t]) for t in range(3)
    ]
    for load in loads:
        load.start()
    for t in (2, 1, 0):
        grad_loads[t].start()

    barrier = pltpu.get_barrier_semaphore()
    for r in range(1, DEVS):
        pl.semaphore_signal(
            barrier, inc=1, device_id_type=MESH,
            device_id=(zs[r // 32] + ys[r // 8 % 4], xs[r // 2 % 4] + cores[r % 2]),
        )

    loads[0].wait()
    lane = lax.broadcasted_iota(jnp.int32, (1, ROWS), 1)
    named = lax.broadcasted_iota(jnp.int32, (DEVS, ROWS), 0)
    hits = []
    for t in range(3):
        live = lane < counts_ref[0, t]
        owner = jnp.where(live, owners[t], -1)
        hits.append(jnp.where(named == owner, 1.0, 0.0).astype(BF16))
    hit = jnp.concatenate(hits, axis=0)
    ahead = lax.broadcasted_iota(jnp.int32, (256, 256), 0) < lax.broadcasted_iota(jnp.int32, (256, 256), 1)
    ahead = jnp.where(ahead, 1.0, 0.0).astype(BF16)
    carry = jnp.zeros((3 * DEVS, 1), F32)
    ranks = []
    for c in range(ROWS // 256):
        part = hit[:, c * 256:(c + 1) * 256]
        before = dot(part, ahead) + carry
        mine = part.astype(F32)
        carry = before[:, 255:256] + mine[:, 255:256]
        ranks.append(jnp.sum((before * mine).reshape(3, DEVS, 256), axis=1))
    rank = jnp.concatenate(ranks, axis=1).astype(jnp.int32)
    for t in range(3):
        owner = owners[t]
        dz, dy = ((owner >> 5) - z) & 3, ((owner >> 3) - y) & 3
        dx, dc = ((owner >> 1) - x) & 3, (owner - core) & 1
        chunk = (3 - ((dy >> 1) * 2 + (dx >> 1))) * 2 + dc
        block = chunk * GROUP + dz * 4 + (dy & 1) * 2 + (dx & 1)
        live = lane < counts_ref[0, t]
        targets[t] = jnp.where(live, block * CAP + rank[t:t + 1], -1)

    for load in loads[1:]:
        load.wait()
    wide_t = wide[...].T
    both_t = jnp.concatenate([mid[...], small[...], jnp.zeros((32, ROWS), F32)], axis=0)
    both = both_t.T
    column = lax.broadcasted_iota(jnp.int32, (ROWS, LANES), 1)
    zeros = lambda n: jnp.zeros((n, D), F32)
    tiers = (
        (2, wide_t, wide[...], pw[...], placed_w),
        (1, mid[...], jnp.where(column < 64, both, 0.0),
         jnp.concatenate([pm[...], zeros(64)], axis=0), placed_m),
        (0, small[...], jnp.where(column >= 64, both, 0.0),
         jnp.concatenate([zeros(64), ps[...], zeros(32)], axis=0), placed_s),
    )
    at = 0
    row = lax.broadcasted_iota(jnp.int32, (ROWS, D), 0)
    for t, table_t, table, projection, placed in tiers:
        grad_loads[t].wait()
        masked = jnp.where(row < counts_ref[0, t], grads[t], 0.0)
        g_high, g_low = split(masked)
        e_high, e_low = split(table_t)
        total = dot(e_high, g_high) + (dot(e_low, g_high) + dot(e_high, g_low))
        slabs = table_t.shape[0] // 4
        totals[at:at + slabs] = total[:, :LANES].reshape(slabs, 4, LANES)
        totals[at + slabs:at + 2 * slabs] = total[:, LANES:].reshape(slabs, 4, LANES)
        at += 2 * slabs
        p_high, p_low = split(projection)
        step = dot_nt(g_high, p_high) + (dot_nt(g_low, p_high) + dot_nt(g_high, p_low))
        moved = table - ROW_RATE * step
        high, low = split(moved)
        placed[:, :LANES] = high
        placed[:, LANES:] = low

    pl.semaphore_wait(barrier, DEVS - 1)

    def share_of(ref, p):
        return ref.at[pl.ds(p * SHARE, SHARE)]

    for j in range(1, N_ROWS):
        p = zs[j // 4] + ys[j % 4]
        pltpu.make_async_remote_copy(
            share_of(totals, p), stage1.at[rows_at], red_send.at[0], red_recv.at[0],
            device_id=(p, serve_at), device_id_type=MESH,
        ).start()

    slot_row = lax.broadcasted_iota(jnp.int32, (CHUNK, ROWS), 0)
    column = lax.broadcasted_iota(jnp.int32, (CHUNK, LANES), 1)

    def place(c, carry):
        base = c * CHUNK

        def chosen(t):
            return jnp.where(slot_row == targets[t] - base, 1.0, 0.0).astype(BF16)

        got_a = dot(chosen(2), placed_w[...])
        got_b = dot(chosen(1), placed_m[...]) + dot(chosen(0), placed_s[...])
        a = got_a[:, :LANES] + got_a[:, LANES:]
        b = got_b[:, :LANES] + got_b[:, LANES:]
        size = jnp.abs(b)
        codes = [
            scale_code(jnp.max(part, axis=1, keepdims=True))
            for part in (jnp.abs(a), jnp.where(column < 64, size, 0.0), jnp.where(column >= 64, size, 0.0))
        ]
        a = fixed(a, scale_up(codes[0]))
        b = fixed(b, jnp.where(column < 64, scale_up(codes[1]), scale_up(codes[2])))
        for i, code in enumerate(codes):
            b = jnp.where(column == 96 + i, code, b)
        packed = (a.astype(jnp.int32) << 16) | (b.astype(jnp.int32) & 0xFFFF)
        send[pl.ds(c * GROUP, GROUP)] = packed.reshape(GROUP, 3, 4, LANES)

        left = 3 - c // 2
        y_at = [(y + left // 2 * 2 + d) % 4 for d in range(2)]
        x_at = [(x + left % 2 * 2 + d) % 4 * 2 for d in range(2)]
        core_at = (core + c) % 2
        for w in range(GROUP):
            copy = pltpu.make_async_remote_copy(
                send.at[c * GROUP + w], recv_hbm.at[me], send_sem, recv_sem,
                device_id=(zs[w // 4] + y_at[w // 2 % 2], x_at[w % 2] + core_at), device_id_type=MESH,
            )
            if w == 0:
                pl.when(c != 6)(copy.start)
            else:
                copy.start()
        return carry

    lax.fori_loop(0, CHUNKS, place, 0)
    own = pltpu.make_async_copy(send.at[6 * GROUP], recv_hbm.at[me], own_sem)
    own.start()

    def all_of(ref, n, sem):
        pltpu.make_async_copy(ref.at[pl.ds(0, n)], ref.at[pl.ds(0, n)], sem).wait()

    stage1[rows_at] = totals[pl.ds(rows_at * SHARE, SHARE)]
    all_of(stage1, N_ROWS - 1, red_recv.at[0])
    sum1[...] = jnp.sum(stage1[...], axis=0)
    for j in range(1, N_SERVE):
        pltpu.make_async_remote_copy(
            sum1, stage2.at[serve_at], red_send.at[1], red_recv.at[1],
            device_id=(rows_at, xs[j // 2] + cores[j % 2]), device_id_type=MESH,
        ).start()
    stage2[serve_at] = sum1[...]
    all_of(stage2, N_SERVE - 1, red_recv.at[1])
    full[rows_at] = jnp.sum(stage2[...], axis=0)
    for j in range(1, N_ROWS):
        pltpu.make_async_remote_copy(
            full.at[rows_at], full.at[rows_at], red_send.at[2], red_recv.at[2],
            device_id=(zs[j // 4] + ys[j % 4], serve_at), device_id_type=MESH,
        ).start()
    all_of(full, N_ROWS - 1, red_recv.at[2])

    summed = full[...].reshape(N_ROWS * SHARE * 4, LANES)
    at = 0
    fresh = []
    for projection in (pw[...], pm[...], ps[...]):
        width = projection.shape[0]
        total = jnp.concatenate([summed[at:at + width], summed[at + width:at + 2 * width]], axis=1)
        at += 2 * width
        size = jnp.sum(total * total, axis=(0, 1), keepdims=True)
        fresh.append(projection - (STEP_NORM / jnp.sqrt(size + 1e-06)) * total)
    columns = (
        jnp.concatenate([zeros(64), fresh[2], zeros(32)], axis=0),
        jnp.concatenate([fresh[1], zeros(64)], axis=0),
        fresh[0],
    )
    for t in range(3):
        high, low = split(columns[t])
        weights_ref[0:128, t * D:(t + 1) * D] = high
        weights_ref[128:256, t * D:(t + 1) * D] = high
        weights_ref[256:384, t * D:(t + 1) * D] = low

    own.wait()
    all_of(recv_hbm, DEVS - 1, recv_sem)
    all_of(send, DEVS - 1, send_sem)
    all_of(stage1, N_ROWS - 1, red_send.at[0])
    all_of(stage2, N_SERVE - 1, red_send.at[1])
    all_of(full, N_ROWS - 1, red_send.at[2])


def project_kernel(recv_ref, weights_ref, out_ref):
    packed = recv_ref[...]
    b = (packed << 16) >> 16
    code = b[:, 96:99].astype(F32)
    down = 1.0 / scale_up(code)
    column = lax.broadcasted_iota(jnp.int32, packed.shape, 1)
    a = (packed >> 16).astype(F32) * down[:, 0:1]
    b = b.astype(F32) * jnp.where(column < 64, down[:, 1:2], jnp.where(column < 96, down[:, 2:3], 0.0))
    for rows, first, last in ((b, 0, 2 * D), (a, 2 * D, 3 * D)):
        high, low = split(rows)
        both = jnp.concatenate([high, low, high], axis=1)
        out_ref[:, first:last] = dot(both, weights_ref[:, first:last]).astype(BF16)


def local(rows_small, rows_mid, rows_wide, row_grads, proj_small, proj_mid, proj_wide, counts, owners):
    hbm = pl.BlockSpec(memory_space=pl.ANY)
    vmem = pl.BlockSpec(memory_space=pltpu.VMEM)
    recv, weights = pl.pallas_call(
        front_kernel,
        out_shape=(
            jax.ShapeDtypeStruct((DEVS, 3, 4, LANES), jnp.int32),
            jax.ShapeDtypeStruct((384, 3 * D), BF16),
        ),
        in_specs=[hbm] * 7 + [pl.BlockSpec(memory_space=pltpu.SMEM), hbm],
        out_specs=(hbm, vmem),
        scratch_shapes=[
            pltpu.VMEM((32, ROWS), F32),
            pltpu.VMEM((64, ROWS), F32),
            pltpu.VMEM((ROWS, LANES), F32),
            pltpu.VMEM((3, ROWS, D), F32),
            pltpu.VMEM((32, D), F32),
            pltpu.VMEM((64, D), F32),
            pltpu.VMEM((128, D), F32),
            pltpu.VMEM((3, 1, ROWS), jnp.int32),
            pltpu.VMEM((ROWS, 2 * LANES), BF16),
            pltpu.VMEM((ROWS, 2 * LANES), BF16),
            pltpu.VMEM((ROWS, 2 * LANES), BF16),
            pltpu.VMEM((3, 1, ROWS), jnp.int32),
            pltpu.VMEM((DEVS, 3, 4, LANES), jnp.int32),
            pltpu.VMEM((N_ROWS * SHARE, 4, LANES), F32),
            pltpu.VMEM((N_ROWS, SHARE, 4, LANES), F32),
            pltpu.VMEM((SHARE, 4, LANES), F32),
            pltpu.VMEM((N_SERVE, SHARE, 4, LANES), F32),
            pltpu.VMEM((N_ROWS, SHARE, 4, LANES), F32),
            pltpu.SemaphoreType.DMA((10,)),
            pltpu.SemaphoreType.DMA,
            pltpu.SemaphoreType.DMA,
            pltpu.SemaphoreType.DMA((3,)),
            pltpu.SemaphoreType.DMA((3,)),
            pltpu.SemaphoreType.DMA,
        ],
        compiler_params=pltpu.CompilerParams(
            collective_id=0, has_side_effects=True, vmem_limit_bytes=64 << 20
        ),
        cost_estimate=pl.CostEstimate(flops=4_000_000_000, bytes_accessed=8_000_000, transcendentals=0),
        name="step_and_route",
    )(
        rows_small.T, rows_mid.T, rows_wide, row_grads, proj_small, proj_mid, proj_wide,
        counts.T, jnp.transpose(owners, (0, 2, 1)),
    )
    part = 192
    return pl.pallas_call(
        project_kernel,
        grid=(SLOTS // part,),
        out_shape=jax.ShapeDtypeStruct((SLOTS, 3 * D), BF16),
        in_specs=[
            pl.BlockSpec((part, LANES), lambda i: (i, 0)),
            pl.BlockSpec((384, 3 * D), lambda i: (0, 0)),
        ],
        out_specs=pl.BlockSpec((part, 3 * D), lambda i: (i, 0)),
        compiler_params=pltpu.CompilerParams(vmem_limit_bytes=64 << 20),
        cost_estimate=pl.CostEstimate(flops=1_000_000_000, bytes_accessed=5_000_000, transcendentals=0),
        name="project",
    )(recv.reshape(SLOTS, LANES), weights)


def solution(mesh):
    return jax.shard_map(
        local,
        mesh=mesh,
        in_specs=(
            P(("rows", "serve"), None),
            P(("rows", "serve"), None),
            P(("rows", "serve"), None),
            P(None, ("rows", "serve"), None),
            P(),
            P(),
            P(),
            P(None, ("rows", "serve")),
            P(None, ("rows", "serve"), None),
        ),
        out_specs=P(("rows", "serve"), None),
        check_vma=False,
    )
```

```python
import functools

import jax
import jax.numpy as jnp
from jax import lax
from jax.experimental import pallas as pl
from jax.experimental.pallas import tpu as pltpu
from jax.sharding import PartitionSpec as P

STEP_NORM = 16.0
ROW_RATE = 0.1
MESH = pl.DeviceIdType.MESH
FAR_FIRST = sorted(range(1, 16), key=lambda j: -(min(j // 4, 4 - j // 4) + min(j % 4, 4 - j % 4)))
N_ROWS = 16
N_SERVE = 8
DEVS = 128
CAP = 12
SLOTS = DEVS * CAP
ROWS = 1024
D = 256
LANES = 128
GROUP = 16
CHUNK = GROUP * CAP
CHUNKS = DEVS // GROUP
SHARE = 7
FINE = 64
SELF_GROUP = 6
EARLY = 6
MIDDLE = 8
PARTS = 4
STRIPE = 768
PART = SLOTS // PARTS
F32 = jnp.float32
BF16 = jnp.bfloat16


def split(x):
    high = x.astype(BF16)
    low = (x - high.astype(F32)).astype(BF16)
    return high, low


def dot(a, b):
    return lax.dot_general(a, b, (((1,), (0,)), ((), ())), preferred_element_type=F32)


def dot_nt(a, b):
    return lax.dot_general(a, b, (((1,), (1,)), ((), ())), preferred_element_type=F32)


def scale_code(size):
    code = jnp.ceil(jnp.log2(jnp.maximum(size, 2.0 ** -109)) * FINE)
    return jnp.minimum(jnp.maximum(code, -110.0 * FINE), 128.0 * FINE)


def scale_up(code):
    return jnp.exp2(15.0 - code * (1.0 / FINE))


def fixed(x, factor):
    return jnp.clip(jnp.floor(x * factor + 0.5), -32767.0, 32767.0)


def front_kernel(
    small_hbm, mid_hbm, wide_hbm, grads_hbm, ps_hbm, pm_hbm, pw_hbm, counts_ref, owners_hbm,
    spread_hbm, weights_ref,
    small, mid, wide, grads, ps, pm, pw, owners,
    parts, placed_w, placed_m, placed_s, targets, send, recv, spread, totals, stage1, sum1, stage2, full,
    in_sem, send_sem, recv_sem, red_send, red_recv, own_sem, out_sem,
):
    rows_at = lax.axis_index("rows")
    serve_at = lax.axis_index("serve")
    me = rows_at * N_SERVE + serve_at
    z, y, x, core = rows_at // 4, rows_at % 4, serve_at // 2, serve_at % 2
    zs = [(z + d) % 4 * 4 for d in range(4)]
    ys = [(y + d) % 4 for d in range(4)]
    xs = [(x + d) % 4 * 2 for d in range(4)]
    cores = [core, 1 - core]

    sources = (owners_hbm, small_hbm, mid_hbm, wide_hbm, ps_hbm, pm_hbm, pw_hbm)
    holders = (owners, small, mid, wide, ps, pm, pw)
    loads = [pltpu.make_async_copy(s, h, in_sem.at[i]) for i, (s, h) in enumerate(zip(sources, holders))]
    grad_loads = [
        pltpu.make_async_copy(grads_hbm.at[t], grads.at[t], in_sem.at[len(loads) + t]) for t in range(3)
    ]
    for load in loads[3:4] + grad_loads[2:] + loads[1:3] + grad_loads[1::-1] + loads[4:] + loads[:1]:
        load.start()

    barrier = pltpu.get_barrier_semaphore()
    for r in range(1, DEVS):
        pl.semaphore_signal(
            barrier, inc=1, device_id_type=MESH,
            device_id=(zs[r // 32] + ys[r // 8 % 4], xs[r // 2 % 4] + cores[r % 2]),
        )

    for load in loads[1:]:
        load.wait()
    wide_t = wide[...].T
    both_t = jnp.concatenate([mid[...], small[...], jnp.zeros((32, ROWS), F32)], axis=0)
    both = both_t.T
    column = lax.broadcasted_iota(jnp.int32, (ROWS, LANES), 1)
    zeros = lambda n: jnp.zeros((n, D), F32)
    tiers = (
        (2, wide_t, wide[...], pw[...], placed_w),
        (1, mid[...], jnp.where(column < 64, both, 0.0),
         jnp.concatenate([pm[...], zeros(64)], axis=0), placed_m),
        (0, small[...], jnp.where(column >= 64, both, 0.0),
         jnp.concatenate([zeros(64), ps[...], zeros(32)], axis=0), placed_s),
    )
    at = 0
    row = lax.broadcasted_iota(jnp.int32, (ROWS, D), 0)
    for t, table_t, table, projection, placed in tiers:
        grad_loads[t].wait()
        masked = jnp.where(row < counts_ref[0, t], grads[t], 0.0)
        g_high, g_low = split(masked)
        parts[t, :, :D] = g_high
        parts[t, :, D:] = g_low
        e_high, e_low = split(table_t)
        total = dot(e_high, g_high) + (dot(e_low, g_high) + dot(e_high, g_low))
        slabs = table_t.shape[0] // 4
        totals[at:at + slabs] = total[:, :LANES].reshape(slabs, 4, LANES)
        totals[at + slabs:at + 2 * slabs] = total[:, LANES:].reshape(slabs, 4, LANES)
        at += 2 * slabs

    pl.semaphore_wait(barrier, DEVS - 1)

    def share_of(ref, p):
        return ref.at[pl.ds(p * SHARE, SHARE)]

    for j in FAR_FIRST:
        p = zs[j // 4] + ys[j % 4]
        pltpu.make_async_remote_copy(
            share_of(totals, p), stage1.at[rows_at], red_send.at[0], red_recv.at[0],
            device_id=(p, serve_at), device_id_type=MESH,
        ).start()

    loads[0].wait()
    lane = lax.broadcasted_iota(jnp.int32, (1, ROWS), 1)
    named = lax.broadcasted_iota(jnp.int32, (DEVS, ROWS), 0)
    hits = []
    for t in range(3):
        live = lane < counts_ref[0, t]
        owner = jnp.where(live, owners[t], -1)
        hits.append(jnp.where(named == owner, 1.0, 0.0).astype(BF16))
    hit = jnp.concatenate(hits, axis=0)
    ahead = lax.broadcasted_iota(jnp.int32, (256, 256), 0) < lax.broadcasted_iota(jnp.int32, (256, 256), 1)
    ahead = jnp.where(ahead, 1.0, 0.0).astype(BF16)
    carry = jnp.zeros((3 * DEVS, 1), F32)
    ranks = []
    for c in range(ROWS // 256):
        part = hit[:, c * 256:(c + 1) * 256]
        before = dot(part, ahead) + carry
        mine = part.astype(F32)
        carry = before[:, 255:256] + mine[:, 255:256]
        ranks.append(jnp.sum((before * mine).reshape(3, DEVS, 256), axis=1))
    rank = jnp.concatenate(ranks, axis=1).astype(jnp.int32)
    for t in range(3):
        owner = owners[t]
        dz, dy = ((owner >> 5) - z) & 3, ((owner >> 3) - y) & 3
        dx, dc = ((owner >> 1) - x) & 3, (owner - core) & 1
        chunk = (3 - ((dy >> 1) * 2 + (dx >> 1))) * 2 + dc
        block = chunk * GROUP + dz * 4 + (dy & 1) * 2 + (dx & 1)
        live = lane < counts_ref[0, t]
        targets[t] = jnp.where(live, block * CAP + rank[t:t + 1], -1)

    for t, table_t, table, projection, placed in tiers:
        g_high, g_low = parts[t, :, :D], parts[t, :, D:]
        p_high, p_low = split(projection)
        step = dot_nt(g_high, p_high) + (dot_nt(g_low, p_high) + dot_nt(g_high, p_low))
        moved = table - ROW_RATE * step
        high, low = split(moved)
        placed[:, :LANES] = high
        placed[:, LANES:] = low

    slot_row = lax.broadcasted_iota(jnp.int32, (CHUNK, ROWS), 0)
    column = lax.broadcasted_iota(jnp.int32, (CHUNK, LANES), 1)

    def place(c):
        base = c * CHUNK

        def chosen(t):
            return jnp.where(slot_row == targets[t] - base, 1.0, 0.0).astype(BF16)

        got_a = dot(chosen(2), placed_w[...])
        got_b = dot(chosen(1), placed_m[...]) + dot(chosen(0), placed_s[...])
        a = got_a[:, :LANES] + got_a[:, LANES:]
        b = got_b[:, :LANES] + got_b[:, LANES:]
        size = jnp.abs(b)
        codes = [
            scale_code(jnp.max(part, axis=1, keepdims=True))
            for part in (jnp.abs(a), jnp.where(column < 64, size, 0.0), jnp.where(column >= 64, size, 0.0))
        ]
        a = fixed(a, scale_up(codes[0]))
        b = fixed(b, jnp.where(column < 64, scale_up(codes[1]), scale_up(codes[2])))
        for i, code in enumerate(codes):
            b = jnp.where(column == 96 + i, code, b)
        packed = (a.astype(jnp.int32) << 16) | (b.astype(jnp.int32) & 0xFFFF)
        send[pl.ds(c * GROUP, GROUP)] = packed.reshape(GROUP, 3, 4, LANES)

    def send_group(c):
        left = 3 - c // 2
        y_at = [(y + left // 2 * 2 + d) % 4 for d in range(2)]
        x_at = [(x + left % 2 * 2 + d) % 4 * 2 for d in range(2)]
        core_at = (core + c) % 2
        for w in range(GROUP):
            if c is SELF_GROUP and w == 0:
                continue
            pltpu.make_async_remote_copy(
                send.at[c * GROUP + w], recv.at[me], send_sem, recv_sem,
                device_id=(zs[w // 4] + y_at[w // 2 % 2], x_at[w % 2] + core_at), device_id_type=MESH,
            ).start()

    def place_and_send(c, carry):
        place(c)
        send_group(c)
        return carry

    def place_only(c, carry):
        place(c)
        return carry

    lax.fori_loop(0, EARLY, place_and_send, 0)
    lax.fori_loop(EARLY, CHUNKS, place_only, 0)
    own = pltpu.make_async_copy(send.at[SELF_GROUP * GROUP], recv.at[me], own_sem)
    own.start()

    def all_of(ref, n, sem):
        pltpu.make_async_copy(ref.at[pl.ds(0, n)], ref.at[pl.ds(0, n)], sem).wait()

    stage1[rows_at] = totals[pl.ds(rows_at * SHARE, SHARE)]
    all_of(stage1, N_ROWS - 1, red_recv.at[0])
    sum1[...] = jnp.sum(stage1[...], axis=0)
    for j in (4, 5, 2, 3, 6, 7, 1):
        pltpu.make_async_remote_copy(
            sum1, stage2.at[serve_at], red_send.at[1], red_recv.at[1],
            device_id=(rows_at, xs[j // 2] + cores[j % 2]), device_id_type=MESH,
        ).start()
    for c in range(EARLY, MIDDLE):
        send_group(c)
    stage2[serve_at] = sum1[...]
    all_of(stage2, N_SERVE - 1, red_recv.at[1])
    full[rows_at] = jnp.sum(stage2[...], axis=0)
    for j in FAR_FIRST:
        pltpu.make_async_remote_copy(
            full.at[rows_at], full.at[rows_at], red_send.at[2], red_recv.at[2],
            device_id=(zs[j // 4] + ys[j % 4], serve_at), device_id_type=MESH,
        ).start()
    for c in range(MIDDLE, CHUNKS):
        send_group(c)
    own.wait()
    all_of(recv, DEVS - 1, recv_sem)
    column = lax.broadcasted_iota(jnp.int32, (PART, LANES), 1)
    for i in range(PARTS):
        part = pl.ds(i * PART, PART)
        packed = recv[i * PART // CAP:(i + 1) * PART // CAP].reshape(PART, LANES)
        b = (packed << 16) >> 16
        down = 1.0 / scale_up(b[:, 96:99].astype(F32))
        a = (packed >> 16).astype(F32) * down[:, 0:1]
        b = b.astype(F32) * jnp.where(column < 64, down[:, 1:2], jnp.where(column < 96, down[:, 2:3], 0.0))
        for k, rows in enumerate((a, b)):
            high, low = split(rows)
            spread[k, part, :LANES] = high
            spread[k, part, LANES:] = low
    kept = pltpu.make_async_copy(spread, spread_hbm, out_sem)
    kept.start()

    all_of(full, N_ROWS - 1, red_recv.at[2])

    summed = full[...].reshape(N_ROWS * SHARE * 4, LANES)
    at = 0
    fresh = []
    for projection in (pw[...], pm[...], ps[...]):
        width = projection.shape[0]
        total = jnp.concatenate([summed[at:at + width], summed[at + width:at + 2 * width]], axis=1)
        at += 2 * width
        size = jnp.sum(total * total, axis=(0, 1), keepdims=True)
        fresh.append(projection - (STEP_NORM / jnp.sqrt(size + 1e-06)) * total)
    columns = (
        jnp.concatenate([zeros(64), fresh[2], zeros(32)], axis=0),
        jnp.concatenate([fresh[1], zeros(64)], axis=0),
        fresh[0],
    )
    for t in range(3):
        high, low = split(columns[t])
        weights_ref[0:128, t * D:(t + 1) * D] = high
        weights_ref[128:256, t * D:(t + 1) * D] = low

    kept.wait()
    all_of(send, DEVS - 1, send_sem)
    all_of(stage1, N_ROWS - 1, red_send.at[0])
    all_of(stage2, N_SERVE - 1, red_send.at[1])
    all_of(full, N_ROWS - 1, red_send.at[2])


def project_kernel(spread_ref, weights_ref, out_ref):
    for k, first, last in ((1, 0, 2 * D), (0, 2 * D, 3 * D)):
        high, low = weights_ref[:LANES, first:last], weights_ref[LANES:, first:last]
        both = jnp.concatenate([high, high], axis=0)
        out_ref[:, first:last] = (dot(spread_ref[k], both) + dot(spread_ref[k, :, :LANES], low)).astype(BF16)


def local(rows_small, rows_mid, rows_wide, row_grads, proj_small, proj_mid, proj_wide, counts, owners):
    hbm = pl.BlockSpec(memory_space=pl.ANY)
    vmem = pl.BlockSpec(memory_space=pltpu.VMEM)
    spread, weights = pl.pallas_call(
        front_kernel,
        out_shape=(
            jax.ShapeDtypeStruct((2, SLOTS, 2 * LANES), BF16),
            jax.ShapeDtypeStruct((2 * LANES, 3 * D), BF16),
        ),
        in_specs=[hbm] * 7 + [pl.BlockSpec(memory_space=pltpu.SMEM), hbm],
        out_specs=(hbm, vmem),
        scratch_shapes=[
            pltpu.VMEM((32, ROWS), F32),
            pltpu.VMEM((64, ROWS), F32),
            pltpu.VMEM((ROWS, LANES), F32),
            pltpu.VMEM((3, ROWS, D), F32),
            pltpu.VMEM((32, D), F32),
            pltpu.VMEM((64, D), F32),
            pltpu.VMEM((128, D), F32),
            pltpu.VMEM((3, 1, ROWS), jnp.int32),
            pltpu.VMEM((3, ROWS, 2 * D), BF16),
            pltpu.VMEM((ROWS, 2 * LANES), BF16),
            pltpu.VMEM((ROWS, 2 * LANES), BF16),
            pltpu.VMEM((ROWS, 2 * LANES), BF16),
            pltpu.VMEM((3, 1, ROWS), jnp.int32),
            pltpu.VMEM((DEVS, 3, 4, LANES), jnp.int32),
            pltpu.VMEM((DEVS, 3, 4, LANES), jnp.int32),
            pltpu.VMEM((2, SLOTS, 2 * LANES), BF16),
            pltpu.VMEM((N_ROWS * SHARE, 4, LANES), F32),
            pltpu.VMEM((N_ROWS, SHARE, 4, LANES), F32),
            pltpu.VMEM((SHARE, 4, LANES), F32),
            pltpu.VMEM((N_SERVE, SHARE, 4, LANES), F32),
            pltpu.VMEM((N_ROWS, SHARE, 4, LANES), F32),
            pltpu.SemaphoreType.DMA((10,)),
            pltpu.SemaphoreType.DMA,
            pltpu.SemaphoreType.DMA,
            pltpu.SemaphoreType.DMA((3,)),
            pltpu.SemaphoreType.DMA((3,)),
            pltpu.SemaphoreType.DMA,
            pltpu.SemaphoreType.DMA,
        ],
        compiler_params=pltpu.CompilerParams(
            collective_id=0, has_side_effects=True, vmem_limit_bytes=64 << 20
        ),
        cost_estimate=pl.CostEstimate(flops=4_000_000_000, bytes_accessed=8_000_000, transcendentals=0),
        name="step_and_route",
    )(
        rows_small.T, rows_mid.T, rows_wide, row_grads, proj_small, proj_mid, proj_wide,
        counts.T, jnp.transpose(owners, (0, 2, 1)),
    )
    return pl.pallas_call(
        project_kernel,
        grid=(SLOTS // STRIPE,),
        out_shape=jax.ShapeDtypeStruct((SLOTS, 3 * D), BF16),
        in_specs=[
            pl.BlockSpec((2, STRIPE, 2 * LANES), lambda i: (0, i, 0)),
            pl.BlockSpec((2 * LANES, 3 * D), lambda i: (0, 0)),
        ],
        out_specs=pl.BlockSpec((STRIPE, 3 * D), lambda i: (i, 0)),
        compiler_params=pltpu.CompilerParams(vmem_limit_bytes=64 << 20),
        cost_estimate=pl.CostEstimate(flops=1_000_000_000, bytes_accessed=5_000_000, transcendentals=0),
        name="project",
    )(spread, weights)


def solution(mesh):
    return jax.shard_map(
        local,
        mesh=mesh,
        in_specs=(
            P(("rows", "serve"), None),
            P(("rows", "serve"), None),
            P(("rows", "serve"), None),
            P(None, ("rows", "serve"), None),
            P(),
            P(),
            P(),
            P(None, ("rows", "serve")),
            P(None, ("rows", "serve"), None),
        ),
        out_specs=P(("rows", "serve"), None),
        check_vma=False,
    )
```

```python
import functools

import jax
import jax.numpy as jnp
from jax import lax
from jax.experimental import pallas as pl
from jax.experimental.pallas import tpu as pltpu
from jax.sharding import PartitionSpec as P

STEP_NORM = 16.0
ROW_RATE = 0.1
MESH = pl.DeviceIdType.MESH
FAR_FIRST = sorted(range(1, 16), key=lambda j: -(min(j // 4, 4 - j // 4) + min(j % 4, 4 - j % 4)))
N_ROWS = 16
N_SERVE = 8
DEVS = 128
CAP = 12
SLOTS = DEVS * CAP
ROWS = 1024
D = 256
LANES = 128
GROUP = 32
CHUNK = GROUP * CAP
CHUNKS = DEVS // GROUP
SHARE = 7
FINE = 64
EARLY = 2
STRIPE = 768
PLANE = 8 * CAP
F32 = jnp.float32
BF16 = jnp.bfloat16


def split(x):
    high = x.astype(BF16)
    low = (x - high.astype(F32)).astype(BF16)
    return high, low


def dot(a, b):
    return lax.dot_general(a, b, (((1,), (0,)), ((), ())), preferred_element_type=F32)


def dot_nt(a, b):
    return lax.dot_general(a, b, (((1,), (1,)), ((), ())), preferred_element_type=F32)


def scale_code(size):
    code = jnp.ceil(jnp.log2(jnp.maximum(size, 2.0 ** -109)) * FINE)
    return jnp.minimum(jnp.maximum(code, -110.0 * FINE), 128.0 * FINE)


def scale_up(code):
    return jnp.exp2(15.0 - code * (1.0 / FINE))


def fixed(x, factor):
    return jnp.clip(jnp.floor(x * factor + 0.5), -32767.0, 32767.0)


def front_kernel(
    small_hbm, mid_hbm, wide_hbm, grads_hbm, ps_hbm, pm_hbm, pw_hbm, counts_ref, owners_hbm,
    spread_hbm, weights_ref,
    small, mid, wide, grads, ps, pm, pw, owners,
    parts, placed_w, placed_m, placed_s, targets, send, recv, spread, totals, stage1, sum1, stage2, full,
    in_sem, send_sem, recv_sem, red_send, red_recv, out_sem,
):
    rows_at = lax.axis_index("rows")
    serve_at = lax.axis_index("serve")
    me = rows_at * N_SERVE + serve_at
    z, y, x, core = rows_at // 4, rows_at % 4, serve_at // 2, serve_at % 2
    zs = [(z + d) % 4 * 4 for d in range(4)]
    ys = [(y + d) % 4 for d in range(4)]
    xs = [(x + d) % 4 * 2 for d in range(4)]
    cores = [core, 1 - core]

    sources = (owners_hbm, small_hbm, mid_hbm, wide_hbm, ps_hbm, pm_hbm, pw_hbm)
    holders = (owners, small, mid, wide, ps, pm, pw)
    loads = [pltpu.make_async_copy(s, h, in_sem.at[i]) for i, (s, h) in enumerate(zip(sources, holders))]
    grad_loads = [
        pltpu.make_async_copy(grads_hbm.at[t], grads.at[t], in_sem.at[len(loads) + t]) for t in range(3)
    ]
    for load in (loads[3], grad_loads[2], loads[2], grad_loads[1], loads[1], grad_loads[0], *loads[4:], loads[0]):
        load.start()

    barrier = pltpu.get_barrier_semaphore()
    for r in range(1, DEVS):
        pl.semaphore_signal(
            barrier, inc=1, device_id_type=MESH,
            device_id=(zs[r // 32] + ys[r // 8 % 4], xs[r // 2 % 4] + cores[r % 2]),
        )

    at = 0
    row = lax.broadcasted_iota(jnp.int32, (ROWS, D), 0)
    for t, load, table in ((2, loads[3], wide), (1, loads[2], mid), (0, loads[1], small)):
        load.wait()
        table_t = wide[...].T if t == 2 else table[...]
        width = table_t.shape[0]
        e_high, e_low = split(table_t)
        grad_loads[t].wait()
        masked = jnp.where(row < counts_ref[0, t], grads[t], 0.0)
        g_high, g_low = split(masked)
        parts[t, :, :D] = g_high
        parts[t, :, D:] = g_low
        first = dot(jnp.concatenate([e_high, e_low], axis=0), g_high)
        total = first[:width] + (first[width:] + dot(e_high, g_low))
        slabs = width // 4
        totals[at:at + slabs] = total[:, :LANES].reshape(slabs, 4, LANES)
        totals[at + slabs:at + 2 * slabs] = total[:, LANES:].reshape(slabs, 4, LANES)
        at += 2 * slabs

    loads[0].wait()
    lane = lax.broadcasted_iota(jnp.int32, (1, ROWS), 1)
    named = lax.broadcasted_iota(jnp.int32, (DEVS, ROWS), 0)
    hits = []
    for t in range(3):
        live = lane < counts_ref[0, t]
        owner = jnp.where(live, owners[t], -1)
        hits.append(jnp.where(named == owner, 1.0, 0.0).astype(BF16))
    hit = jnp.concatenate(hits, axis=0)
    ahead = lax.broadcasted_iota(jnp.int32, (256, 256), 0) < lax.broadcasted_iota(jnp.int32, (256, 256), 1)
    ahead = jnp.where(ahead, 1.0, 0.0).astype(BF16)
    carry = jnp.zeros((3 * DEVS, 1), F32)
    ranks = []
    for c in range(ROWS // 256):
        part = hit[:, c * 256:(c + 1) * 256]
        before = dot(part, ahead) + carry
        mine = part.astype(F32)
        carry = before[:, 255:256] + mine[:, 255:256]
        ranks.append(jnp.sum((before * mine).reshape(3, DEVS, 256), axis=1))
    rank = jnp.concatenate(ranks, axis=1).astype(jnp.int32)
    for t in range(3):
        owner = owners[t]
        dz, dy = ((owner >> 5) - z) & 3, ((owner >> 3) - y) & 3
        dx, dc = ((owner >> 1) - x) & 3, (owner - core) & 1
        chunk = (dy - dz - 1) & 3
        block = chunk * GROUP + dz * 8 + dx * 2 + dc
        live = lane < counts_ref[0, t]
        targets[t] = jnp.where(live, block * CAP + rank[t:t + 1], -1)

    pl.semaphore_wait(barrier, DEVS - 1)

    def share_of(ref, p):
        return ref.at[pl.ds(p * SHARE, SHARE)]

    for j in FAR_FIRST:
        p = zs[j // 4] + ys[j % 4]
        pltpu.make_async_remote_copy(
            share_of(totals, p), stage1.at[rows_at], red_send.at[0], red_recv.at[0],
            device_id=(p, serve_at), device_id_type=MESH,
        ).start()

    for load in loads[4:]:
        load.wait()
    both = jnp.concatenate([mid[...], small[...], jnp.zeros((32, ROWS), F32)], axis=0).T
    column = lax.broadcasted_iota(jnp.int32, (ROWS, LANES), 1)
    zeros = lambda n: jnp.zeros((n, D), F32)
    tiers = (
        (2, wide[...], pw[...], placed_w),
        (1, jnp.where(column < 64, both, 0.0), jnp.concatenate([pm[...], zeros(64)], axis=0), placed_m),
        (0, jnp.where(column >= 64, both, 0.0), jnp.concatenate([zeros(64), ps[...], zeros(32)], axis=0), placed_s),
    )
    for t, table, projection, placed in tiers:
        g_high, g_low = parts[t, :, :D], parts[t, :, D:]
        p_high, p_low = split(projection)
        step = dot_nt(g_high, jnp.concatenate([p_high, p_low], axis=0))
        step = step[:, :LANES] + (step[:, LANES:] + dot_nt(g_low, p_high))
        high, low = split(table - ROW_RATE * step)
        placed[:, :LANES] = high
        placed[:, LANES:] = low

    slot_row = lax.broadcasted_iota(jnp.int32, (CHUNK, ROWS), 0)
    column = lax.broadcasted_iota(jnp.int32, (CHUNK, LANES), 1)
    of_mid = (column < 64) | (column == 97)

    def place(c):
        base = c * CHUNK

        def chosen(t):
            return jnp.where(slot_row == targets[t] - base, 1.0, 0.0).astype(BF16)

        got_a = dot(chosen(2), placed_w[...])
        got_b = dot(chosen(1), placed_m[...]) + dot(chosen(0), placed_s[...])
        a = got_a[:, :LANES] + got_a[:, LANES:]
        b = got_b[:, :LANES] + got_b[:, LANES:]
        size = jnp.abs(b)
        largest = lambda part: jnp.max(part, axis=1, keepdims=True)
        size_a = largest(jnp.abs(a))
        size_m, size_s = largest(jnp.where(column < 64, size, 0.0)), largest(jnp.where(column >= 64, size, 0.0))
        code_a = scale_code(size_a)
        code_b = scale_code(jnp.where(of_mid, size_m, size_s))
        a = fixed(a, scale_up(code_a))
        b = fixed(b, scale_up(code_b))
        b = jnp.where(column < 96, b, jnp.where(column == 96, code_a, code_b))
        packed = (a.astype(jnp.int32) << 16) | (b.astype(jnp.int32) & 0xFFFF)
        send[pl.ds(c * GROUP, GROUP)] = packed.reshape(GROUP, 3, 4, LANES)

    def send_group(c):
        for dz in range(4):
            row_to = zs[dz] + (y + dz + c + 1) % 4
            for r in range(8):
                if c is CHUNKS - 1 and dz == 0 and r == 0:
                    continue
                pltpu.make_async_remote_copy(
                    send.at[c * GROUP + dz * 8 + r], recv.at[me], send_sem, recv_sem.at[c],
                    device_id=(row_to, xs[r // 2] + cores[r % 2]), device_id_type=MESH,
                ).start()

    def place_and_send(c, carry):
        place(c)
        send_group(c)
        return carry

    def place_only(c, carry):
        place(c)
        return carry

    lax.fori_loop(0, EARLY, place_and_send, 0)
    lax.fori_loop(EARLY, CHUNKS, place_only, 0)
    own = pltpu.make_async_copy(send.at[(CHUNKS - 1) * GROUP], recv.at[me], recv_sem.at[CHUNKS - 1])
    own.start()

    def all_of(ref, n, sem):
        pltpu.make_async_copy(ref.at[pl.ds(0, n)], ref.at[pl.ds(0, n)], sem).wait()

    stage1[rows_at] = totals[pl.ds(rows_at * SHARE, SHARE)]
    all_of(stage1, N_ROWS - 1, red_recv.at[0])
    sum1[...] = jnp.sum(stage1[...], axis=0)
    for j in (4, 5, 2, 3, 6, 7, 1):
        pltpu.make_async_remote_copy(
            sum1, stage2.at[serve_at], red_send.at[1], red_recv.at[1],
            device_id=(rows_at, xs[j // 2] + cores[j % 2]), device_id_type=MESH,
        ).start()
    for c in range(EARLY, CHUNKS):
        send_group(c)
    stage2[serve_at] = sum1[...]
    all_of(stage2, N_SERVE - 1, red_recv.at[1])
    full[rows_at] = jnp.sum(stage2[...], axis=0)
    for j in FAR_FIRST:
        pltpu.make_async_remote_copy(
            full.at[rows_at], full.at[rows_at], red_send.at[2], red_recv.at[2],
            device_id=(zs[j // 4] + ys[j % 4], serve_at), device_id_type=MESH,
        ).start()
    column = lax.broadcasted_iota(jnp.int32, (PLANE, LANES), 1)

    def decode(n, carry):
        c, dz = n // 4, n % 4
        plane = (z + 4 - dz) % 4 * 4 + (y + 7 - dz - c) % 4

        @pl.when(dz == 0)
        def _():
            all_of(recv, GROUP, recv_sem.at[c])

        packed = recv[pl.ds(plane * 8, 8)].reshape(PLANE, LANES)
        b = (packed << 16) >> 16
        down = 1.0 / scale_up(b[:, 96:99].astype(F32))
        a = (packed >> 16).astype(F32) * down[:, 0:1]
        b = b.astype(F32) * jnp.where(column < 64, down[:, 1:2], jnp.where(column < 96, down[:, 2:3], 0.0))
        at = pl.ds(pl.multiple_of(plane * PLANE, PLANE), PLANE)
        for k, rows in enumerate((a, b)):
            high, low = split(rows)
            spread[k, at, :LANES] = high
            spread[k, at, LANES:] = low
        pltpu.make_async_copy(spread.at[:, at], spread_hbm.at[:, at], out_sem).start()
        return carry

    lax.fori_loop(0, N_ROWS, decode, 0)

    all_of(full, N_ROWS - 1, red_recv.at[2])

    summed = full[...].reshape(N_ROWS * SHARE * 4, LANES)
    at = 0
    fresh = []
    for projection in (pw[...], pm[...], ps[...]):
        width = projection.shape[0]
        total = jnp.concatenate([summed[at:at + width], summed[at + width:at + 2 * width]], axis=1)
        at += 2 * width
        size = jnp.sum(total * total, axis=(0, 1), keepdims=True)
        fresh.append(projection - (STEP_NORM / jnp.sqrt(size + 1e-06)) * total)
    columns = (
        jnp.concatenate([zeros(64), fresh[2], zeros(32)], axis=0),
        jnp.concatenate([fresh[1], zeros(64)], axis=0),
        fresh[0],
    )
    for t in range(3):
        high, low = split(columns[t])
        weights_ref[0:128, t * D:(t + 1) * D] = high
        weights_ref[128:256, t * D:(t + 1) * D] = low

    pltpu.make_async_copy(spread, spread_hbm, out_sem).wait()
    all_of(send, DEVS - 1, send_sem)
    all_of(stage1, N_ROWS - 1, red_send.at[0])
    all_of(stage2, N_SERVE - 1, red_send.at[1])
    all_of(full, N_ROWS - 1, red_send.at[2])


def project_kernel(spread_ref, weights_ref, out_ref):
    for k, first, last in ((1, 0, 2 * D), (0, 2 * D, 3 * D)):
        high, low = weights_ref[:LANES, first:last], weights_ref[LANES:, first:last]
        both = jnp.concatenate([high, high], axis=0)
        out_ref[:, first:last] = (dot(spread_ref[k], both) + dot(spread_ref[k, :, :LANES], low)).astype(BF16)


def local(rows_small, rows_mid, rows_wide, row_grads, proj_small, proj_mid, proj_wide, counts, owners):
    hbm = pl.BlockSpec(memory_space=pl.ANY)
    vmem = pl.BlockSpec(memory_space=pltpu.VMEM)
    spread, weights = pl.pallas_call(
        front_kernel,
        out_shape=(
            jax.ShapeDtypeStruct((2, SLOTS, 2 * LANES), BF16),
            jax.ShapeDtypeStruct((2 * LANES, 3 * D), BF16),
        ),
        in_specs=[hbm] * 7 + [pl.BlockSpec(memory_space=pltpu.SMEM), hbm],
        out_specs=(hbm, vmem),
        scratch_shapes=[
            pltpu.VMEM((32, ROWS), F32),
            pltpu.VMEM((64, ROWS), F32),
            pltpu.VMEM((ROWS, LANES), F32),
            pltpu.VMEM((3, ROWS, D), F32),
            pltpu.VMEM((32, D), F32),
            pltpu.VMEM((64, D), F32),
            pltpu.VMEM((128, D), F32),
            pltpu.VMEM((3, 1, ROWS), jnp.int32),
            pltpu.VMEM((3, ROWS, 2 * D), BF16),
            pltpu.VMEM((ROWS, 2 * LANES), BF16),
            pltpu.VMEM((ROWS, 2 * LANES), BF16),
            pltpu.VMEM((ROWS, 2 * LANES), BF16),
            pltpu.VMEM((3, 1, ROWS), jnp.int32),
            pltpu.VMEM((DEVS, 3, 4, LANES), jnp.int32),
            pltpu.VMEM((DEVS, 3, 4, LANES), jnp.int32),
            pltpu.VMEM((2, SLOTS, 2 * LANES), BF16),
            pltpu.VMEM((N_ROWS * SHARE, 4, LANES), F32),
            pltpu.VMEM((N_ROWS, SHARE, 4, LANES), F32),
            pltpu.VMEM((SHARE, 4, LANES), F32),
            pltpu.VMEM((N_SERVE, SHARE, 4, LANES), F32),
            pltpu.VMEM((N_ROWS, SHARE, 4, LANES), F32),
            pltpu.SemaphoreType.DMA((10,)),
            pltpu.SemaphoreType.DMA,
            pltpu.SemaphoreType.DMA((CHUNKS,)),
            pltpu.SemaphoreType.DMA((3,)),
            pltpu.SemaphoreType.DMA((3,)),
            pltpu.SemaphoreType.DMA,
        ],
        compiler_params=pltpu.CompilerParams(
            collective_id=0, has_side_effects=True, vmem_limit_bytes=64 << 20
        ),
        cost_estimate=pl.CostEstimate(flops=4_000_000_000, bytes_accessed=8_000_000, transcendentals=0),
        name="step_and_route",
    )(
        rows_small.T, rows_mid.T, rows_wide, row_grads, proj_small, proj_mid, proj_wide,
        counts.T, jnp.transpose(owners, (0, 2, 1)),
    )
    return pl.pallas_call(
        project_kernel,
        grid=(SLOTS // STRIPE,),
        out_shape=jax.ShapeDtypeStruct((SLOTS, 3 * D), BF16),
        in_specs=[
            pl.BlockSpec((2, STRIPE, 2 * LANES), lambda i: (0, i, 0)),
            pl.BlockSpec((2 * LANES, 3 * D), lambda i: (0, 0)),
        ],
        out_specs=pl.BlockSpec((STRIPE, 3 * D), lambda i: (i, 0)),
        compiler_params=pltpu.CompilerParams(vmem_limit_bytes=64 << 20),
        cost_estimate=pl.CostEstimate(flops=1_000_000_000, bytes_accessed=5_000_000, transcendentals=0),
        name="project",
    )(spread, weights)


def solution(mesh):
    return jax.shard_map(
        local,
        mesh=mesh,
        in_specs=(
            P(("rows", "serve"), None),
            P(("rows", "serve"), None),
            P(("rows", "serve"), None),
            P(None, ("rows", "serve"), None),
            P(),
            P(),
            P(),
            P(None, ("rows", "serve")),
            P(None, ("rows", "serve"), None),
        ),
        out_specs=P(("rows", "serve"), None),
        check_vma=False,
    )
```

```python
import functools

import jax
import jax.numpy as jnp
from jax import lax
from jax.experimental import pallas as pl
from jax.experimental.pallas import tpu as pltpu
from jax.sharding import PartitionSpec as P

STEP_NORM = 16.0
ROW_RATE = 0.1
MESH = pl.DeviceIdType.MESH
ALL_FAR_FIRST = sorted(
    range(1, 128), key=lambda r: -sum(min(d, 4 - d) for d in (r // 32, r // 8 % 4, r // 2 % 4))
)
FAR_FIRST = sorted(range(1, 16), key=lambda j: -(min(j // 4, 4 - j // 4) + min(j % 4, 4 - j % 4)))
N_ROWS = 16
N_SERVE = 8
DEVS = 128
CAP = 12
SLOTS = DEVS * CAP
ROWS = 1024
D = 256
LANES = 128
GROUP = 32
CHUNK = GROUP * CAP
CHUNKS = DEVS // GROUP
SHARE = 7
FINE = 64
EARLY = 2
STRIPE = 768
PLANE = 8 * CAP
F32 = jnp.float32
BF16 = jnp.bfloat16


def split(x):
    high = x.astype(BF16)
    low = (x - high.astype(F32)).astype(BF16)
    return high, low


def dot(a, b):
    return lax.dot_general(a, b, (((1,), (0,)), ((), ())), preferred_element_type=F32)


def dot_nt(a, b):
    return lax.dot_general(a, b, (((1,), (1,)), ((), ())), preferred_element_type=F32)


def scale_code(size):
    code = jnp.ceil(jnp.log2(jnp.maximum(size, 2.0 ** -109)) * FINE)
    return jnp.minimum(jnp.maximum(code, -110.0 * FINE), 128.0 * FINE)


def scale_up(code):
    return jnp.exp2(15.0 - code * (1.0 / FINE))


def fixed(x, factor):
    return jnp.clip(jnp.floor(x * factor + 0.5), -32767.0, 32767.0)


def front_kernel(
    small_hbm, mid_hbm, wide_hbm, grads_hbm, ps_hbm, pm_hbm, pw_hbm, counts_ref, owners_hbm,
    spread_hbm, weights_hbm,
    small, mid, wide, grads, ps, pm, pw, owners,
    parts, placed_w, placed_m, placed_s, targets, send, recv, spread, weights_ref, totals, stage1, sum1, stage2, full,
    in_sem, send_sem, recv_sem, red_send, red_recv, out_sem, w_sem,
):
    rows_at = lax.axis_index("rows")
    serve_at = lax.axis_index("serve")
    me = rows_at * N_SERVE + serve_at
    z, y, x, core = rows_at // 4, rows_at % 4, serve_at // 2, serve_at % 2
    zs = [(z + d) % 4 * 4 for d in range(4)]
    ys = [(y + d) % 4 for d in range(4)]
    xs = [(x + d) % 4 * 2 for d in range(4)]
    cores = [core, 1 - core]

    sources = (owners_hbm, small_hbm, mid_hbm, wide_hbm, ps_hbm, pm_hbm, pw_hbm)
    holders = (owners, small, mid, wide, ps, pm, pw)
    loads = [pltpu.make_async_copy(s, h, in_sem.at[i]) for i, (s, h) in enumerate(zip(sources, holders))]
    grad_loads = [
        pltpu.make_async_copy(grads_hbm.at[t], grads.at[t], in_sem.at[len(loads) + t]) for t in range(3)
    ]
    for load in (loads[3], grad_loads[2], loads[2], grad_loads[1], loads[1], grad_loads[0], *loads[4:], loads[0]):
        load.start()

    barrier = pltpu.get_barrier_semaphore()
    for r in ALL_FAR_FIRST:
        pl.semaphore_signal(
            barrier, inc=1, device_id_type=MESH,
            device_id=(zs[r // 32] + ys[r // 8 % 4], xs[r // 2 % 4] + cores[r % 2]),
        )

    at = 0
    row = lax.broadcasted_iota(jnp.int32, (ROWS, D), 0)
    for t, load, table in ((2, loads[3], wide), (1, loads[2], mid), (0, loads[1], small)):
        load.wait()
        table_t = wide[...].T if t == 2 else table[...]
        width = table_t.shape[0]
        e_high, e_low = split(table_t)
        grad_loads[t].wait()
        masked = jnp.where(row < counts_ref[0, t], grads[t], 0.0)
        g_high, g_low = split(masked)
        parts[t, :, :D] = g_high
        parts[t, :, D:] = g_low
        first = dot(jnp.concatenate([e_high, e_low], axis=0), g_high)
        total = first[:width] + (first[width:] + dot(e_high, g_low))
        slabs = width // 4
        totals[at:at + slabs] = total[:, :LANES].reshape(slabs, 4, LANES)
        totals[at + slabs:at + 2 * slabs] = total[:, LANES:].reshape(slabs, 4, LANES)
        at += 2 * slabs

    loads[0].wait()
    lane = lax.broadcasted_iota(jnp.int32, (1, ROWS), 1)
    named = lax.broadcasted_iota(jnp.int32, (DEVS, ROWS), 0)
    hits = []
    for t in range(3):
        live = lane < counts_ref[0, t]
        owner = jnp.where(live, owners[t], -1)
        hits.append(jnp.where(named == owner, 1.0, 0.0).astype(BF16))
    hit = jnp.concatenate(hits, axis=0)
    ahead = lax.broadcasted_iota(jnp.int32, (256, 256), 0) < lax.broadcasted_iota(jnp.int32, (256, 256), 1)
    ahead = jnp.where(ahead, 1.0, 0.0).astype(BF16)
    carry = jnp.zeros((3 * DEVS, 1), F32)
    ranks = []
    for c in range(ROWS // 256):
        part = hit[:, c * 256:(c + 1) * 256]
        before = dot(part, ahead) + carry
        mine = part.astype(F32)
        carry = before[:, 255:256] + mine[:, 255:256]
        ranks.append(jnp.sum((before * mine).reshape(3, DEVS, 256), axis=1))
    rank = jnp.concatenate(ranks, axis=1).astype(jnp.int32)
    for t in range(3):
        owner = owners[t]
        dz, dy = ((owner >> 5) - z) & 3, ((owner >> 3) - y) & 3
        dx, dc = ((owner >> 1) - x) & 3, (owner - core) & 1
        chunk = (dy - dz - 1) & 3
        block = chunk * GROUP + dz * 8 + dx * 2 + dc
        live = lane < counts_ref[0, t]
        targets[t] = jnp.where(live, block * CAP + rank[t:t + 1], -1)

    pl.semaphore_wait(barrier, DEVS - 1)

    def share_of(ref, p):
        return ref.at[pl.ds(p * SHARE, SHARE)]

    for j in FAR_FIRST:
        p = zs[j // 4] + ys[j % 4]
        pltpu.make_async_remote_copy(
            share_of(totals, p), stage1.at[rows_at], red_send.at[0], red_recv.at[0],
            device_id=(p, serve_at), device_id_type=MESH,
        ).start()

    for load in loads[4:]:
        load.wait()
    both = jnp.concatenate([mid[...], small[...], jnp.zeros((32, ROWS), F32)], axis=0).T
    column = lax.broadcasted_iota(jnp.int32, (ROWS, LANES), 1)
    zeros = lambda n: jnp.zeros((n, D), F32)
    tiers = (
        (2, wide[...], pw[...], placed_w),
        (1, jnp.where(column < 64, both, 0.0), jnp.concatenate([pm[...], zeros(64)], axis=0), placed_m),
        (0, jnp.where(column >= 64, both, 0.0), jnp.concatenate([zeros(64), ps[...], zeros(32)], axis=0), placed_s),
    )
    for t, table, projection, placed in tiers:
        g_high, g_low = parts[t, :, :D], parts[t, :, D:]
        p_high, p_low = split(projection)
        step = dot_nt(g_high, jnp.concatenate([p_high, p_low], axis=0))
        step = step[:, :LANES] + (step[:, LANES:] + dot_nt(g_low, p_high))
        high, low = split(table - ROW_RATE * step)
        placed[:, :LANES] = high
        placed[:, LANES:] = low

    slot_row = lax.broadcasted_iota(jnp.int32, (CHUNK, ROWS), 0)
    column = lax.broadcasted_iota(jnp.int32, (CHUNK, LANES), 1)
    of_mid = (column < 64) | (column == 97)

    def place(c):
        base = c * CHUNK

        def chosen(t):
            return jnp.where(slot_row == targets[t] - base, 1.0, 0.0).astype(BF16)

        got_a = dot(chosen(2), placed_w[...])
        got_b = dot(chosen(1), placed_m[...]) + dot(chosen(0), placed_s[...])
        a = got_a[:, :LANES] + got_a[:, LANES:]
        b = got_b[:, :LANES] + got_b[:, LANES:]
        size = jnp.abs(b)
        largest = lambda part: jnp.max(part, axis=1, keepdims=True)
        size_a = largest(jnp.abs(a))
        size_m, size_s = largest(jnp.where(column < 64, size, 0.0)), largest(jnp.where(column >= 64, size, 0.0))
        code_a = scale_code(size_a)
        code_b = scale_code(jnp.where(of_mid, size_m, size_s))
        a = fixed(a, scale_up(code_a))
        b = fixed(b, scale_up(code_b))
        b = jnp.where(column < 96, b, jnp.where(column == 96, code_a, code_b))
        packed = (a.astype(jnp.int32) << 16) | (b.astype(jnp.int32) & 0xFFFF)
        send[pl.ds(c * GROUP, GROUP)] = packed.reshape(GROUP, 3, 4, LANES)

    def send_group(c):
        for dz in range(4):
            row_to = zs[dz] + (y + dz + c + 1) % 4
            for r in range(8):
                if c is CHUNKS - 1 and dz == 0 and r == 0:
                    continue
                pltpu.make_async_remote_copy(
                    send.at[c * GROUP + dz * 8 + r], recv.at[me], send_sem, recv_sem.at[c],
                    device_id=(row_to, xs[r // 2] + cores[r % 2]), device_id_type=MESH,
                ).start()

    def place_and_send(c, carry):
        place(c)
        send_group(c)
        return carry

    def place_only(c, carry):
        place(c)
        return carry

    lax.fori_loop(0, EARLY, place_and_send, 0)
    lax.fori_loop(EARLY, CHUNKS, place_only, 0)
    own = pltpu.make_async_copy(send.at[(CHUNKS - 1) * GROUP], recv.at[me], recv_sem.at[CHUNKS - 1])
    own.start()

    def all_of(ref, n, sem):
        pltpu.make_async_copy(ref.at[pl.ds(0, n)], ref.at[pl.ds(0, n)], sem).wait()

    stage1[rows_at] = totals[pl.ds(rows_at * SHARE, SHARE)]
    all_of(stage1, N_ROWS - 1, red_recv.at[0])
    sum1[...] = jnp.sum(stage1[...], axis=0)
    for j in (4, 5, 2, 3, 6, 7, 1):
        pltpu.make_async_remote_copy(
            sum1, stage2.at[serve_at], red_send.at[1], red_recv.at[1],
            device_id=(rows_at, xs[j // 2] + cores[j % 2]), device_id_type=MESH,
        ).start()
    for c in range(EARLY, CHUNKS):
        send_group(c)
    stage2[serve_at] = sum1[...]
    all_of(stage2, N_SERVE - 1, red_recv.at[1])
    full[rows_at] = jnp.sum(stage2[...], axis=0)
    for j in FAR_FIRST:
        pltpu.make_async_remote_copy(
            full.at[rows_at], full.at[rows_at], red_send.at[2], red_recv.at[2],
            device_id=(zs[j // 4] + ys[j % 4], serve_at), device_id_type=MESH,
        ).start()
    column = lax.broadcasted_iota(jnp.int32, (PLANE, LANES), 1)

    def decode(n, carry):
        c, dz = n // 4, n % 4
        plane = (z + 4 - dz) % 4 * 4 + (y + 7 - dz - c) % 4

        @pl.when(dz == 0)
        def _():
            all_of(recv, GROUP, recv_sem.at[c])

        packed = recv[pl.ds(plane * 8, 8)].reshape(PLANE, LANES)
        b = (packed << 16) >> 16
        down = 1.0 / scale_up(b[:, 96:99].astype(F32))
        a = (packed >> 16).astype(F32) * down[:, 0:1]
        b = b.astype(F32) * jnp.where(column < 64, down[:, 1:2], jnp.where(column < 96, down[:, 2:3], 0.0))
        at = pl.ds(pl.multiple_of(plane * PLANE, PLANE), PLANE)
        for k, rows in enumerate((a, b)):
            high, low = split(rows)
            spread[k, at, :LANES] = high
            spread[k, at, LANES:] = low
        pltpu.make_async_copy(spread.at[:, at], spread_hbm.at[:, at], out_sem).start()
        return carry

    lax.fori_loop(0, 16, decode, 0)

    all_of(full, N_ROWS - 1, red_recv.at[2])

    summed = full[...].reshape(N_ROWS * SHARE * 4, LANES)
    at = 0
    fresh = []
    for projection in (pw[...], pm[...], ps[...]):
        width = projection.shape[0]
        total = jnp.concatenate([summed[at:at + width], summed[at + width:at + 2 * width]], axis=1)
        at += 2 * width
        size = jnp.sum(total * total, axis=(0, 1), keepdims=True)
        fresh.append(projection - (STEP_NORM / jnp.sqrt(size + 1e-06)) * total)
    columns = (
        jnp.concatenate([zeros(64), fresh[2], zeros(32)], axis=0),
        jnp.concatenate([fresh[1], zeros(64)], axis=0),
        fresh[0],
    )
    for t in range(3):
        high, low = split(columns[t])
        weights_ref[0:128, t * D:(t + 1) * D] = high
        weights_ref[128:256, t * D:(t + 1) * D] = low

    weights_out = pltpu.make_async_copy(weights_ref, weights_hbm, w_sem)
    weights_out.start()
    weights_out.wait()
    pltpu.make_async_copy(spread, spread_hbm, out_sem).wait()
    all_of(send, DEVS - 1, send_sem)
    all_of(stage1, N_ROWS - 1, red_send.at[0])
    all_of(stage2, N_SERVE - 1, red_send.at[1])
    all_of(full, N_ROWS - 1, red_send.at[2])


def project_kernel(spread_ref, weights_ref, out_ref):
    for k, first, last in ((1, 0, 2 * D), (0, 2 * D, 3 * D)):
        high, low = weights_ref[:LANES, first:last], weights_ref[LANES:, first:last]
        both = jnp.concatenate([high, high], axis=0)
        out_ref[:, first:last] = (dot(spread_ref[k], both) + dot(spread_ref[k, :, :LANES], low)).astype(BF16)


def local(rows_small, rows_mid, rows_wide, row_grads, proj_small, proj_mid, proj_wide, counts, owners):
    hbm = pl.BlockSpec(memory_space=pl.ANY)
    spread, weights = pl.pallas_call(
        front_kernel,
        out_shape=(
            jax.ShapeDtypeStruct((2, SLOTS, 2 * LANES), BF16),
            jax.ShapeDtypeStruct((2 * LANES, 3 * D), BF16),
        ),
        in_specs=[hbm] * 7 + [pl.BlockSpec(memory_space=pltpu.SMEM), hbm],
        out_specs=(hbm, hbm),
        scratch_shapes=[
            pltpu.VMEM((32, ROWS), F32),
            pltpu.VMEM((64, ROWS), F32),
            pltpu.VMEM((ROWS, LANES), F32),
            pltpu.VMEM((3, ROWS, D), F32),
            pltpu.VMEM((32, D), F32),
            pltpu.VMEM((64, D), F32),
            pltpu.VMEM((128, D), F32),
            pltpu.VMEM((3, 1, ROWS), jnp.int32),
            pltpu.VMEM((3, ROWS, 2 * D), BF16),
            pltpu.VMEM((ROWS, 2 * LANES), BF16),
            pltpu.VMEM((ROWS, 2 * LANES), BF16),
            pltpu.VMEM((ROWS, 2 * LANES), BF16),
            pltpu.VMEM((3, 1, ROWS), jnp.int32),
            pltpu.VMEM((DEVS, 3, 4, LANES), jnp.int32),
            pltpu.VMEM((DEVS, 3, 4, LANES), jnp.int32),
            pltpu.VMEM((2, SLOTS, 2 * LANES), BF16),
            pltpu.VMEM((2 * LANES, 3 * D), BF16),
            pltpu.VMEM((N_ROWS * SHARE, 4, LANES), F32),
            pltpu.VMEM((N_ROWS, SHARE, 4, LANES), F32),
            pltpu.VMEM((SHARE, 4, LANES), F32),
            pltpu.VMEM((N_SERVE, SHARE, 4, LANES), F32),
            pltpu.VMEM((N_ROWS, SHARE, 4, LANES), F32),
            pltpu.SemaphoreType.DMA((10,)),
            pltpu.SemaphoreType.DMA,
            pltpu.SemaphoreType.DMA((CHUNKS,)),
            pltpu.SemaphoreType.DMA((3,)),
            pltpu.SemaphoreType.DMA((3,)),
            pltpu.SemaphoreType.DMA,
            pltpu.SemaphoreType.DMA,
        ],
        compiler_params=pltpu.CompilerParams(
            collective_id=0, has_side_effects=True, vmem_limit_bytes=64 << 20
        ),
        cost_estimate=pl.CostEstimate(flops=4_000_000_000, bytes_accessed=8_000_000, transcendentals=0),
        name="step_and_route",
    )(
        rows_small.T, rows_mid.T, rows_wide, row_grads, proj_small, proj_mid, proj_wide,
        counts.T, jnp.transpose(owners, (0, 2, 1)),
    )
    return pl.pallas_call(
        project_kernel,
        grid=(SLOTS // STRIPE,),
        out_shape=jax.ShapeDtypeStruct((SLOTS, 3 * D), BF16),
        in_specs=[
            pl.BlockSpec((2, STRIPE, 2 * LANES), lambda i: (0, i, 0)),
            pl.BlockSpec((2 * LANES, 3 * D), lambda i: (0, 0)),
        ],
        out_specs=pl.BlockSpec((STRIPE, 3 * D), lambda i: (i, 0)),
        compiler_params=pltpu.CompilerParams(vmem_limit_bytes=64 << 20),
        cost_estimate=pl.CostEstimate(flops=1_000_000_000, bytes_accessed=5_000_000, transcendentals=0),
        name="project",
    )(spread, weights)


def solution(mesh):
    return jax.shard_map(
        local,
        mesh=mesh,
        in_specs=(
            P(("rows", "serve"), None),
            P(("rows", "serve"), None),
            P(("rows", "serve"), None),
            P(None, ("rows", "serve"), None),
            P(),
            P(),
            P(),
            P(None, ("rows", "serve")),
            P(None, ("rows", "serve"), None),
        ),
        out_specs=P(("rows", "serve"), None),
        check_vma=False,
    )
```

```python
import functools

import jax
import jax.numpy as jnp
from jax import lax
from jax.experimental import pallas as pl
from jax.experimental.pallas import tpu as pltpu
from jax.sharding import PartitionSpec as P

STEP_NORM = 16.0
ROW_RATE = 0.1
MESH = pl.DeviceIdType.MESH
ALL_FAR_FIRST = sorted(
    range(1, 128), key=lambda r: -sum(min(d, 4 - d) for d in (r // 32, r // 8 % 4, r // 2 % 4))
)
FAR_FIRST = sorted(range(1, 16), key=lambda j: -(min(j // 4, 4 - j // 4) + min(j % 4, 4 - j % 4)))
N_ROWS = 16
N_SERVE = 8
DEVS = 128
CAP = 12
SLOTS = DEVS * CAP
ROWS = 1024
D = 256
LANES = 128
GROUP = 32
CHUNK = GROUP * CAP
CHUNKS = DEVS // GROUP
SHARE = 7
FINE = 64
SELF_GROUP = 2
EARLY = 2
STRIPE = 768
PLANE = 8 * CAP
F32 = jnp.float32
BF16 = jnp.bfloat16


def split(x):
    high = x.astype(BF16)
    low = (x - high.astype(F32)).astype(BF16)
    return high, low


def dot(a, b):
    return lax.dot_general(a, b, (((1,), (0,)), ((), ())), preferred_element_type=F32)


def dot_nt(a, b):
    return lax.dot_general(a, b, (((1,), (1,)), ((), ())), preferred_element_type=F32)


def scale_code(size):
    code = jnp.ceil(jnp.log2(jnp.maximum(size, 2.0 ** -109)) * FINE)
    return jnp.minimum(jnp.maximum(code, -110.0 * FINE), 128.0 * FINE)


def scale_up(code):
    return jnp.exp2(15.0 - code * (1.0 / FINE))


def fixed(x, factor):
    return jnp.clip(jnp.floor(x * factor + 0.5), -32767.0, 32767.0)


def front_kernel(
    small_hbm, mid_hbm, wide_hbm, grads_hbm, ps_hbm, pm_hbm, pw_hbm, counts_ref, owners_hbm,
    spread_hbm, weights_hbm,
    small, mid, wide, grads, ps, pm, pw, owners,
    parts, placed_w, placed_m, placed_s, targets, send, recv, spread, weights_ref, totals, stage1, sum1, stage2, full,
    in_sem, send_sem, recv_sem, red_send, red_recv, out_sem, w_sem,
):
    rows_at = lax.axis_index("rows")
    serve_at = lax.axis_index("serve")
    me = rows_at * N_SERVE + serve_at
    z, y, x, core = rows_at // 4, rows_at % 4, serve_at // 2, serve_at % 2
    zs = [(z + d) % 4 * 4 for d in range(4)]
    ys = [(y + d) % 4 for d in range(4)]
    xs = [(x + d) % 4 * 2 for d in range(4)]
    cores = [core, 1 - core]

    sources = (owners_hbm, small_hbm, mid_hbm, wide_hbm, ps_hbm, pm_hbm, pw_hbm)
    holders = (owners, small, mid, wide, ps, pm, pw)
    loads = [pltpu.make_async_copy(s, h, in_sem.at[i]) for i, (s, h) in enumerate(zip(sources, holders))]
    grad_loads = [
        pltpu.make_async_copy(grads_hbm.at[t], grads.at[t], in_sem.at[len(loads) + t]) for t in range(3)
    ]
    for load in (loads[3], grad_loads[2], loads[2], grad_loads[1], loads[1], grad_loads[0], *loads[4:], loads[0]):
        load.start()

    barrier = pltpu.get_barrier_semaphore()
    for r in ALL_FAR_FIRST:
        pl.semaphore_signal(
            barrier, inc=1, device_id_type=MESH,
            device_id=(zs[r // 32] + ys[r // 8 % 4], xs[r // 2 % 4] + cores[r % 2]),
        )

    at = 0
    row = lax.broadcasted_iota(jnp.int32, (ROWS, D), 0)
    for t, load, table in ((2, loads[3], wide), (1, loads[2], mid), (0, loads[1], small)):
        load.wait()
        table_t = wide[...].T if t == 2 else table[...]
        width = table_t.shape[0]
        e_high, e_low = split(table_t)
        grad_loads[t].wait()
        masked = jnp.where(row < counts_ref[0, t], grads[t], 0.0)
        g_high, g_low = split(masked)
        parts[t, :, :D] = g_high
        parts[t, :, D:] = g_low
        first = dot(jnp.concatenate([e_high, e_low], axis=0), g_high)
        total = first[:width] + (first[width:] + dot(e_high, g_low))
        slabs = width // 4
        totals[at:at + slabs] = total[:, :LANES].reshape(slabs, 4, LANES)
        totals[at + slabs:at + 2 * slabs] = total[:, LANES:].reshape(slabs, 4, LANES)
        at += 2 * slabs

    loads[0].wait()
    lane = lax.broadcasted_iota(jnp.int32, (1, ROWS), 1)
    named = lax.broadcasted_iota(jnp.int32, (DEVS, ROWS), 0)
    hits = []
    for t in range(3):
        live = lane < counts_ref[0, t]
        owner = jnp.where(live, owners[t], -1)
        hits.append(jnp.where(named == owner, 1.0, 0.0).astype(BF16))
    hit = jnp.concatenate(hits, axis=0)
    ahead = lax.broadcasted_iota(jnp.int32, (256, 256), 0) < lax.broadcasted_iota(jnp.int32, (256, 256), 1)
    ahead = jnp.where(ahead, 1.0, 0.0).astype(BF16)
    carry = jnp.zeros((3 * DEVS, 1), F32)
    ranks = []
    for c in range(ROWS // 256):
        part = hit[:, c * 256:(c + 1) * 256]
        before = dot(part, ahead) + carry
        mine = part.astype(F32)
        carry = before[:, 255:256] + mine[:, 255:256]
        ranks.append(jnp.sum((before * mine).reshape(3, DEVS, 256), axis=1))
    rank = jnp.concatenate(ranks, axis=1).astype(jnp.int32)
    for t in range(3):
        owner = owners[t]
        dz, dy = ((owner >> 5) - z) & 3, ((owner >> 3) - y) & 3
        dx, dc = ((owner >> 1) - x) & 3, (owner - core) & 1
        apart = (dy - dz) & 3
        chunk = jnp.where((apart & 1) == 1, apart >> 1, 2 + (apart >> 1))
        block = chunk * GROUP + dz * 8 + dx * 2 + dc
        live = lane < counts_ref[0, t]
        targets[t] = jnp.where(live, block * CAP + rank[t:t + 1], -1)

    pl.semaphore_wait(barrier, DEVS - 1)

    def share_of(ref, p):
        return ref.at[pl.ds(p * SHARE, SHARE)]

    for j in FAR_FIRST:
        p = zs[j // 4] + ys[j % 4]
        pltpu.make_async_remote_copy(
            share_of(totals, p), stage1.at[rows_at], red_send.at[0], red_recv.at[0],
            device_id=(p, serve_at), device_id_type=MESH,
        ).start()

    for load in loads[4:]:
        load.wait()
    both = jnp.concatenate([mid[...], small[...], jnp.zeros((32, ROWS), F32)], axis=0).T
    column = lax.broadcasted_iota(jnp.int32, (ROWS, LANES), 1)
    zeros = lambda n: jnp.zeros((n, D), F32)
    tiers = (
        (2, wide[...], pw[...], placed_w),
        (1, jnp.where(column < 64, both, 0.0), jnp.concatenate([pm[...], zeros(64)], axis=0), placed_m),
        (0, jnp.where(column >= 64, both, 0.0), jnp.concatenate([zeros(64), ps[...], zeros(32)], axis=0), placed_s),
    )
    for t, table, projection, placed in tiers:
        g_high, g_low = parts[t, :, :D], parts[t, :, D:]
        p_high, p_low = split(projection)
        step = dot_nt(g_high, jnp.concatenate([p_high, p_low], axis=0))
        step = step[:, :LANES] + (step[:, LANES:] + dot_nt(g_low, p_high))
        high, low = split(table - ROW_RATE * step)
        placed[:, :LANES] = high
        placed[:, LANES:] = low

    slot_row = lax.broadcasted_iota(jnp.int32, (CHUNK, ROWS), 0)
    column = lax.broadcasted_iota(jnp.int32, (CHUNK, LANES), 1)
    of_mid = (column < 64) | (column == 97)

    def place(c):
        base = c * CHUNK

        def chosen(t):
            return jnp.where(slot_row == targets[t] - base, 1.0, 0.0).astype(BF16)

        got_a = dot(chosen(2), placed_w[...])
        got_b = dot(chosen(1), placed_m[...]) + dot(chosen(0), placed_s[...])
        a = got_a[:, :LANES] + got_a[:, LANES:]
        b = got_b[:, :LANES] + got_b[:, LANES:]
        size = jnp.abs(b)
        largest = lambda part: jnp.max(part, axis=1, keepdims=True)
        size_a = largest(jnp.abs(a))
        size_m, size_s = largest(jnp.where(column < 64, size, 0.0)), largest(jnp.where(column >= 64, size, 0.0))
        code_a = scale_code(size_a)
        code_b = scale_code(jnp.where(of_mid, size_m, size_s))
        a = fixed(a, scale_up(code_a))
        b = fixed(b, scale_up(code_b))
        b = jnp.where(column < 96, b, jnp.where(column == 96, code_a, code_b))
        packed = (a.astype(jnp.int32) << 16) | (b.astype(jnp.int32) & 0xFFFF)
        send[pl.ds(c * GROUP, GROUP)] = packed.reshape(GROUP, 3, 4, LANES)

    def apart_of(c):
        return jnp.where(c < 2, 1 + 2 * c, 2 * c - 4)

    def send_group(c):
        for dz in (2, 1, 3, 0):
            row_to = zs[dz] + (y + dz + apart_of(c)) % 4
            for r in (4, 5, 2, 3, 6, 7, 0, 1):
                if c is SELF_GROUP and dz == 0 and r == 0:
                    continue
                pltpu.make_async_remote_copy(
                    send.at[c * GROUP + dz * 8 + r], recv.at[me], send_sem, recv_sem.at[c],
                    device_id=(row_to, xs[r // 2] + cores[r % 2]), device_id_type=MESH,
                ).start()

    def place_and_send(c, carry):
        place(c)
        send_group(c)
        return carry

    def place_only(c, carry):
        place(c)
        return carry

    lax.fori_loop(0, EARLY, place_and_send, 0)
    lax.fori_loop(EARLY, CHUNKS, place_only, 0)
    own = pltpu.make_async_copy(send.at[SELF_GROUP * GROUP], recv.at[me], recv_sem.at[SELF_GROUP])
    own.start()

    def all_of(ref, n, sem):
        pltpu.make_async_copy(ref.at[pl.ds(0, n)], ref.at[pl.ds(0, n)], sem).wait()

    stage1[rows_at] = totals[pl.ds(rows_at * SHARE, SHARE)]
    all_of(stage1, N_ROWS - 1, red_recv.at[0])
    sum1[...] = jnp.sum(stage1[...], axis=0)
    for j in (4, 5, 2, 3, 6, 7, 1):
        pltpu.make_async_remote_copy(
            sum1, stage2.at[serve_at], red_send.at[1], red_recv.at[1],
            device_id=(rows_at, xs[j // 2] + cores[j % 2]), device_id_type=MESH,
        ).start()
    for c in range(EARLY, CHUNKS):
        send_group(c)
    stage2[serve_at] = sum1[...]
    all_of(stage2, N_SERVE - 1, red_recv.at[1])
    full[rows_at] = jnp.sum(stage2[...], axis=0)
    for j in FAR_FIRST:
        pltpu.make_async_remote_copy(
            full.at[rows_at], full.at[rows_at], red_send.at[2], red_recv.at[2],
            device_id=(zs[j // 4] + ys[j % 4], serve_at), device_id_type=MESH,
        ).start()
    column = lax.broadcasted_iota(jnp.int32, (PLANE, LANES), 1)

    def decode(c, dz):
        plane = (z + 4 - dz) % 4 * 4 + (y + 8 - dz - apart_of(c)) % 4

        packed = recv[pl.ds(plane * 8, 8)].reshape(PLANE, LANES)
        b = (packed << 16) >> 16
        down = 1.0 / scale_up(b[:, 96:99].astype(F32))
        a = (packed >> 16).astype(F32) * down[:, 0:1]
        b = b.astype(F32) * jnp.where(column < 64, down[:, 1:2], jnp.where(column < 96, down[:, 2:3], 0.0))
        at = pl.ds(pl.multiple_of(plane * PLANE, PLANE), PLANE)
        for k, rows in enumerate((a, b)):
            high, low = split(rows)
            spread[k, at, :LANES] = high
            spread[k, at, LANES:] = low
        pltpu.make_async_copy(spread.at[:, at], spread_hbm.at[:, at], out_sem).start()

    def decode_group(c, carry):
        all_of(recv, GROUP, recv_sem.at[c])
        for dz in range(4):
            decode(c, dz)
        return carry

    lax.fori_loop(0, CHUNKS, decode_group, 0)

    all_of(full, N_ROWS - 1, red_recv.at[2])

    summed = full[...].reshape(N_ROWS * SHARE * 4, LANES)
    at = 0
    fresh = []
    for projection in (pw[...], pm[...], ps[...]):
        width = projection.shape[0]
        total = jnp.concatenate([summed[at:at + width], summed[at + width:at + 2 * width]], axis=1)
        at += 2 * width
        size = jnp.sum(total * total, axis=(0, 1), keepdims=True)
        fresh.append(projection - (STEP_NORM / jnp.sqrt(size + 1e-06)) * total)
    columns = (
        jnp.concatenate([zeros(64), fresh[2], zeros(32)], axis=0),
        jnp.concatenate([fresh[1], zeros(64)], axis=0),
        fresh[0],
    )
    for t in range(3):
        high, low = split(columns[t])
        weights_ref[0:128, t * D:(t + 1) * D] = high
        weights_ref[128:256, t * D:(t + 1) * D] = low

    weights_out = pltpu.make_async_copy(weights_ref, weights_hbm, w_sem)
    weights_out.start()
    weights_out.wait()
    pltpu.make_async_copy(spread, spread_hbm, out_sem).wait()
    all_of(send, DEVS - 1, send_sem)
    all_of(stage1, N_ROWS - 1, red_send.at[0])
    all_of(stage2, N_SERVE - 1, red_send.at[1])
    all_of(full, N_ROWS - 1, red_send.at[2])


def project_kernel(spread_ref, weights_ref, out_ref):
    for k, first, last in ((1, 0, 2 * D), (0, 2 * D, 3 * D)):
        high, low = weights_ref[:LANES, first:last], weights_ref[LANES:, first:last]
        both = jnp.concatenate([high, high], axis=0)
        out_ref[:, first:last] = (dot(spread_ref[k], both) + dot(spread_ref[k, :, :LANES], low)).astype(BF16)


def local(rows_small, rows_mid, rows_wide, row_grads, proj_small, proj_mid, proj_wide, counts, owners):
    hbm = pl.BlockSpec(memory_space=pl.ANY)
    spread, weights = pl.pallas_call(
        front_kernel,
        out_shape=(
            jax.ShapeDtypeStruct((2, SLOTS, 2 * LANES), BF16),
            jax.ShapeDtypeStruct((2 * LANES, 3 * D), BF16),
        ),
        in_specs=[hbm] * 7 + [pl.BlockSpec(memory_space=pltpu.SMEM), hbm],
        out_specs=(hbm, hbm),
        scratch_shapes=[
            pltpu.VMEM((32, ROWS), F32),
            pltpu.VMEM((64, ROWS), F32),
            pltpu.VMEM((ROWS, LANES), F32),
            pltpu.VMEM((3, ROWS, D), F32),
            pltpu.VMEM((32, D), F32),
            pltpu.VMEM((64, D), F32),
            pltpu.VMEM((128, D), F32),
            pltpu.VMEM((3, 1, ROWS), jnp.int32),
            pltpu.VMEM((3, ROWS, 2 * D), BF16),
            pltpu.VMEM((ROWS, 2 * LANES), BF16),
            pltpu.VMEM((ROWS, 2 * LANES), BF16),
            pltpu.VMEM((ROWS, 2 * LANES), BF16),
            pltpu.VMEM((3, 1, ROWS), jnp.int32),
            pltpu.VMEM((DEVS, 3, 4, LANES), jnp.int32),
            pltpu.VMEM((DEVS, 3, 4, LANES), jnp.int32),
            pltpu.VMEM((2, SLOTS, 2 * LANES), BF16),
            pltpu.VMEM((2 * LANES, 3 * D), BF16),
            pltpu.VMEM((N_ROWS * SHARE, 4, LANES), F32),
            pltpu.VMEM((N_ROWS, SHARE, 4, LANES), F32),
            pltpu.VMEM((SHARE, 4, LANES), F32),
            pltpu.VMEM((N_SERVE, SHARE, 4, LANES), F32),
            pltpu.VMEM((N_ROWS, SHARE, 4, LANES), F32),
            pltpu.SemaphoreType.DMA((10,)),
            pltpu.SemaphoreType.DMA,
            pltpu.SemaphoreType.DMA((CHUNKS,)),
            pltpu.SemaphoreType.DMA((3,)),
            pltpu.SemaphoreType.DMA((3,)),
            pltpu.SemaphoreType.DMA,
            pltpu.SemaphoreType.DMA,
        ],
        compiler_params=pltpu.CompilerParams(
            collective_id=0, has_side_effects=True, vmem_limit_bytes=64 << 20
        ),
        cost_estimate=pl.CostEstimate(flops=4_000_000_000, bytes_accessed=8_000_000, transcendentals=0),
        name="step_and_route",
    )(
        rows_small.T, rows_mid.T, rows_wide, row_grads, proj_small, proj_mid, proj_wide,
        counts.T, jnp.transpose(owners, (0, 2, 1)),
    )
    return pl.pallas_call(
        project_kernel,
        grid=(SLOTS // STRIPE,),
        out_shape=jax.ShapeDtypeStruct((SLOTS, 3 * D), BF16),
        in_specs=[
            pl.BlockSpec((2, STRIPE, 2 * LANES), lambda i: (0, i, 0)),
            pl.BlockSpec((2 * LANES, 3 * D), lambda i: (0, 0)),
        ],
        out_specs=pl.BlockSpec((STRIPE, 3 * D), lambda i: (i, 0)),
        compiler_params=pltpu.CompilerParams(vmem_limit_bytes=64 << 20),
        cost_estimate=pl.CostEstimate(flops=1_000_000_000, bytes_accessed=5_000_000, transcendentals=0),
        name="project",
    )(spread, weights)


def solution(mesh):
    return jax.shard_map(
        local,
        mesh=mesh,
        in_specs=(
            P(("rows", "serve"), None),
            P(("rows", "serve"), None),
            P(("rows", "serve"), None),
            P(None, ("rows", "serve"), None),
            P(),
            P(),
            P(),
            P(None, ("rows", "serve")),
            P(None, ("rows", "serve"), None),
        ),
        out_specs=P(("rows", "serve"), None),
        check_vma=False,
    )
```

```python
import functools

import jax
import jax.numpy as jnp
from jax import lax
from jax.experimental import pallas as pl
from jax.experimental.pallas import tpu as pltpu
from jax.sharding import PartitionSpec as P

STEP_NORM = 16.0
ROW_RATE = 0.1
MESH = pl.DeviceIdType.MESH
ALL_FAR_FIRST = sorted(
    range(1, 128), key=lambda r: -sum(min(d, 4 - d) for d in (r // 32, r // 8 % 4, r // 2 % 4))
)
FAR_FIRST = sorted(range(1, 16), key=lambda j: -(min(j // 4, 4 - j // 4) + min(j % 4, 4 - j % 4)))
N_ROWS = 16
N_SERVE = 8
DEVS = 128
CAP = 12
SLOTS = DEVS * CAP
ROWS = 1024
D = 256
LANES = 128
GROUP = 32
CHUNK = GROUP * CAP
CHUNKS = DEVS // GROUP
SHARE = 7
FINE = 64
SELF_GROUP = 2
EARLY = 2
STRIPE = 768
PLANE = 8 * CAP
F32 = jnp.float32
BF16 = jnp.bfloat16


def split(x):
    high = x.astype(BF16)
    low = (x - high.astype(F32)).astype(BF16)
    return high, low


def dot(a, b):
    return lax.dot_general(a, b, (((1,), (0,)), ((), ())), preferred_element_type=F32)


def dot_nt(a, b):
    return lax.dot_general(a, b, (((1,), (1,)), ((), ())), preferred_element_type=F32)


def scale_code(size):
    code = jnp.ceil(jnp.log2(jnp.maximum(size, 2.0 ** -109)) * FINE)
    return jnp.minimum(jnp.maximum(code, -110.0 * FINE), 128.0 * FINE)


def scale_up(code):
    return jnp.exp2(15.0 - code * (1.0 / FINE))


def fixed(x, factor):
    return jnp.clip(jnp.floor(x * factor + 0.5), -32767.0, 32767.0)


def front_kernel(
    small_hbm, mid_hbm, wide_hbm, grads_hbm, ps_hbm, pm_hbm, pw_hbm, counts_ref, owners_hbm,
    spread_hbm, weights_hbm,
    small, mid, wide, grads, ps, pm, pw, owners,
    parts, placed_w, placed_m, placed_s, targets, send, recv, spread, weights_ref, totals, stage1, sum1, stage2, full,
    in_sem, send_sem, recv_sem, red_send, red_recv, out_sem, w_sem,
):
    rows_at = lax.axis_index("rows")
    serve_at = lax.axis_index("serve")
    me = rows_at * N_SERVE + serve_at
    z, y, x, core = rows_at // 4, rows_at % 4, serve_at // 2, serve_at % 2
    zs = [(z + d) % 4 * 4 for d in range(4)]
    ys = [(y + d) % 4 for d in range(4)]
    xs = [(x + d) % 4 * 2 for d in range(4)]
    cores = [core, 1 - core]

    sources = (owners_hbm, small_hbm, mid_hbm, wide_hbm, ps_hbm, pm_hbm, pw_hbm)
    holders = (owners, small, mid, wide, ps, pm, pw)
    loads = [pltpu.make_async_copy(s, h, in_sem.at[i]) for i, (s, h) in enumerate(zip(sources, holders))]
    grad_loads = [
        pltpu.make_async_copy(grads_hbm.at[t], grads.at[t], in_sem.at[len(loads) + t]) for t in range(3)
    ]
    loads[3].start()
    grad_loads[2].start()
    barrier = pltpu.get_barrier_semaphore()
    for r in ALL_FAR_FIRST:
        pl.semaphore_signal(
            barrier, inc=1, device_id_type=MESH,
            device_id=(zs[r // 32] + ys[r // 8 % 4], xs[r // 2 % 4] + cores[r % 2]),
        )

    for load in (loads[2], grad_loads[1], loads[1], grad_loads[0], *loads[4:], loads[0]):
        load.start()

    at = 0
    row = lax.broadcasted_iota(jnp.int32, (ROWS, D), 0)
    for t, load, table in ((2, loads[3], wide), (1, loads[2], mid), (0, loads[1], small)):
        load.wait()
        table_t = wide[...].T if t == 2 else table[...]
        width = table_t.shape[0]
        e_high, e_low = split(table_t)
        grad_loads[t].wait()
        masked = jnp.where(row < counts_ref[0, t], grads[t], 0.0)
        g_high, g_low = split(masked)
        parts[t, :, :D] = g_high
        parts[t, :, D:] = g_low
        first = dot(jnp.concatenate([e_high, e_low], axis=0), g_high)
        total = first[:width] + (first[width:] + dot(e_high, g_low))
        slabs = width // 4
        totals[at:at + slabs] = total[:, :LANES].reshape(slabs, 4, LANES)
        totals[at + slabs:at + 2 * slabs] = total[:, LANES:].reshape(slabs, 4, LANES)
        at += 2 * slabs

    loads[0].wait()
    lane = lax.broadcasted_iota(jnp.int32, (1, ROWS), 1)
    named = lax.broadcasted_iota(jnp.int32, (DEVS, ROWS), 0)
    hits = []
    for t in range(3):
        live = lane < counts_ref[0, t]
        owner = jnp.where(live, owners[t], -1)
        hits.append(jnp.where(named == owner, 1.0, 0.0).astype(BF16))
    hit = jnp.concatenate(hits, axis=0)
    ahead = lax.broadcasted_iota(jnp.int32, (256, 256), 0) < lax.broadcasted_iota(jnp.int32, (256, 256), 1)
    ahead = jnp.where(ahead, 1.0, 0.0).astype(BF16)
    carry = jnp.zeros((3 * DEVS, 1), F32)
    ranks = []
    for c in range(ROWS // 256):
        part = hit[:, c * 256:(c + 1) * 256]
        before = dot(part, ahead) + carry
        mine = part.astype(F32)
        carry = before[:, 255:256] + mine[:, 255:256]
        ranks.append(jnp.sum((before * mine).reshape(3, DEVS, 256), axis=1))
    rank = jnp.concatenate(ranks, axis=1).astype(jnp.int32)
    for t in range(3):
        owner = owners[t]
        dz, dy = ((owner >> 5) - z) & 3, ((owner >> 3) - y) & 3
        dx, dc = ((owner >> 1) - x) & 3, (owner - core) & 1
        apart = (dy - dz) & 3
        chunk = jnp.where((apart & 1) == 1, apart >> 1, 2 + (apart >> 1))
        block = chunk * GROUP + dz * 8 + dx * 2 + dc
        live = lane < counts_ref[0, t]
        targets[t] = jnp.where(live, block * CAP + rank[t:t + 1], -1)

    pl.semaphore_wait(barrier, DEVS - 1)

    def share_of(ref, p):
        return ref.at[pl.ds(p * SHARE, SHARE)]

    for j in FAR_FIRST:
        p = zs[j // 4] + ys[j % 4]
        pltpu.make_async_remote_copy(
            share_of(totals, p), stage1.at[rows_at], red_send.at[0], red_recv.at[0],
            device_id=(p, serve_at), device_id_type=MESH,
        ).start()

    for load in loads[4:]:
        load.wait()
    both = jnp.concatenate([mid[...], small[...], jnp.zeros((32, ROWS), F32)], axis=0).T
    column = lax.broadcasted_iota(jnp.int32, (ROWS, LANES), 1)
    zeros = lambda n: jnp.zeros((n, D), F32)
    tiers = (
        (2, wide[...], pw[...], placed_w),
        (1, jnp.where(column < 64, both, 0.0), jnp.concatenate([pm[...], zeros(64)], axis=0), placed_m),
        (0, jnp.where(column >= 64, both, 0.0), jnp.concatenate([zeros(64), ps[...], zeros(32)], axis=0), placed_s),
    )
    for t, table, projection, placed in tiers:
        g_high, g_low = parts[t, :, :D], parts[t, :, D:]
        p_high, p_low = split(projection)
        step = dot_nt(g_high, jnp.concatenate([p_high, p_low], axis=0))
        step = step[:, :LANES] + (step[:, LANES:] + dot_nt(g_low, p_high))
        high, low = split(table - ROW_RATE * step)
        placed[:, :LANES] = high
        placed[:, LANES:] = low

    slot_row = lax.broadcasted_iota(jnp.int32, (CHUNK, ROWS), 0)
    column = lax.broadcasted_iota(jnp.int32, (CHUNK, LANES), 1)
    of_mid = (column < 64) | (column == 97)

    def place(c):
        base = c * CHUNK

        def chosen(t):
            return jnp.where(slot_row == targets[t] - base, 1.0, 0.0).astype(BF16)

        got_a = dot(chosen(2), placed_w[...])
        got_b = dot(chosen(1), placed_m[...]) + dot(chosen(0), placed_s[...])
        a = got_a[:, :LANES] + got_a[:, LANES:]
        b = got_b[:, :LANES] + got_b[:, LANES:]
        size = jnp.abs(b)
        largest = lambda part: jnp.max(part, axis=1, keepdims=True)
        size_a = largest(jnp.abs(a))
        size_m, size_s = largest(jnp.where(column < 64, size, 0.0)), largest(jnp.where(column >= 64, size, 0.0))
        code_a = scale_code(size_a)
        code_b = scale_code(jnp.where(of_mid, size_m, size_s))
        a = fixed(a, scale_up(code_a))
        b = fixed(b, scale_up(code_b))
        b = jnp.where(column < 96, b, jnp.where(column == 96, code_a, code_b))
        packed = (a.astype(jnp.int32) << 16) | (b.astype(jnp.int32) & 0xFFFF)
        send[pl.ds(c * GROUP, GROUP)] = packed.reshape(GROUP, 3, 4, LANES)

    def apart_of(c):
        return jnp.where(c < 2, 1 + 2 * c, 2 * c - 4)

    def send_group(c):
        for dz in (2, 1, 3, 0):
            row_to = zs[dz] + (y + dz + apart_of(c)) % 4
            for r in (4, 5, 2, 3, 6, 7, 0, 1):
                if c is SELF_GROUP and dz == 0 and r == 0:
                    continue
                pltpu.make_async_remote_copy(
                    send.at[c * GROUP + dz * 8 + r], recv.at[me], send_sem, recv_sem.at[c],
                    device_id=(row_to, xs[r // 2] + cores[r % 2]), device_id_type=MESH,
                ).start()

    def place_and_send(c, carry):
        place(c)
        send_group(c)
        return carry

    def place_only(c, carry):
        place(c)
        return carry

    lax.fori_loop(0, EARLY, place_and_send, 0)
    lax.fori_loop(EARLY, CHUNKS, place_only, 0)
    own = pltpu.make_async_copy(send.at[SELF_GROUP * GROUP], recv.at[me], recv_sem.at[SELF_GROUP])
    own.start()

    def all_of(ref, n, sem):
        pltpu.make_async_copy(ref.at[pl.ds(0, n)], ref.at[pl.ds(0, n)], sem).wait()

    stage1[rows_at] = totals[pl.ds(rows_at * SHARE, SHARE)]
    all_of(stage1, N_ROWS - 1, red_recv.at[0])
    sum1[...] = jnp.sum(stage1[...], axis=0)
    for j in (4, 5, 2, 3, 6, 7, 1):
        pltpu.make_async_remote_copy(
            sum1, stage2.at[serve_at], red_send.at[1], red_recv.at[1],
            device_id=(rows_at, xs[j // 2] + cores[j % 2]), device_id_type=MESH,
        ).start()
    for c in range(EARLY, CHUNKS):
        send_group(c)
    stage2[serve_at] = sum1[...]
    all_of(stage2, N_SERVE - 1, red_recv.at[1])
    full[rows_at] = jnp.sum(stage2[...], axis=0)
    for j in FAR_FIRST:
        pltpu.make_async_remote_copy(
            full.at[rows_at], full.at[rows_at], red_send.at[2], red_recv.at[2],
            device_id=(zs[j // 4] + ys[j % 4], serve_at), device_id_type=MESH,
        ).start()
    column = lax.broadcasted_iota(jnp.int32, (PLANE, LANES), 1)

    def decode(c, dz):
        plane = (z + 4 - dz) % 4 * 4 + (y + 8 - dz - apart_of(c)) % 4

        packed = recv[pl.ds(plane * 8, 8)].reshape(PLANE, LANES)
        b = (packed << 16) >> 16
        down = 1.0 / scale_up(b[:, 96:99].astype(F32))
        a = (packed >> 16).astype(F32) * down[:, 0:1]
        b = b.astype(F32) * jnp.where(column < 64, down[:, 1:2], jnp.where(column < 96, down[:, 2:3], 0.0))
        at = pl.ds(pl.multiple_of(plane * PLANE, PLANE), PLANE)
        for k, rows in enumerate((a, b)):
            high, low = split(rows)
            spread[k, at, :LANES] = high
            spread[k, at, LANES:] = low
        pltpu.make_async_copy(spread.at[:, at], spread_hbm.at[:, at], out_sem).start()

    def decode_group(c, carry):
        all_of(recv, GROUP, recv_sem.at[c])
        for dz in range(4):
            decode(c, dz)
        return carry

    lax.fori_loop(0, CHUNKS, decode_group, 0)

    all_of(full, N_ROWS - 1, red_recv.at[2])

    summed = full[...].reshape(N_ROWS * SHARE * 4, LANES)
    at = 0
    fresh = []
    for projection in (pw[...], pm[...], ps[...]):
        width = projection.shape[0]
        total = jnp.concatenate([summed[at:at + width], summed[at + width:at + 2 * width]], axis=1)
        at += 2 * width
        size = jnp.sum(total * total, axis=(0, 1), keepdims=True)
        fresh.append(projection - (STEP_NORM / jnp.sqrt(size + 1e-06)) * total)
    columns = (
        jnp.concatenate([zeros(64), fresh[2], zeros(32)], axis=0),
        jnp.concatenate([fresh[1], zeros(64)], axis=0),
        fresh[0],
    )
    for t in range(3):
        high, low = split(columns[t])
        weights_ref[0:128, t * D:(t + 1) * D] = high
        weights_ref[128:256, t * D:(t + 1) * D] = low

    weights_out = pltpu.make_async_copy(weights_ref, weights_hbm, w_sem)
    weights_out.start()
    weights_out.wait()
    pltpu.make_async_copy(spread, spread_hbm, out_sem).wait()
    all_of(send, DEVS - 1, send_sem)
    all_of(stage1, N_ROWS - 1, red_send.at[0])
    all_of(stage2, N_SERVE - 1, red_send.at[1])
    all_of(full, N_ROWS - 1, red_send.at[2])


def project_kernel(spread_ref, weights_ref, out_ref):
    for k, first, last in ((1, 0, 2 * D), (0, 2 * D, 3 * D)):
        high, low = weights_ref[:LANES, first:last], weights_ref[LANES:, first:last]
        both = jnp.concatenate([high, high], axis=0)
        out_ref[:, first:last] = (dot(spread_ref[k], both) + dot(spread_ref[k, :, :LANES], low)).astype(BF16)


def local(rows_small, rows_mid, rows_wide, row_grads, proj_small, proj_mid, proj_wide, counts, owners):
    hbm = pl.BlockSpec(memory_space=pl.ANY)
    spread, weights = pl.pallas_call(
        front_kernel,
        out_shape=(
            jax.ShapeDtypeStruct((2, SLOTS, 2 * LANES), BF16),
            jax.ShapeDtypeStruct((2 * LANES, 3 * D), BF16),
        ),
        in_specs=[hbm] * 7 + [pl.BlockSpec(memory_space=pltpu.SMEM), hbm],
        out_specs=(hbm, hbm),
        scratch_shapes=[
            pltpu.VMEM((32, ROWS), F32),
            pltpu.VMEM((64, ROWS), F32),
            pltpu.VMEM((ROWS, LANES), F32),
            pltpu.VMEM((3, ROWS, D), F32),
            pltpu.VMEM((32, D), F32),
            pltpu.VMEM((64, D), F32),
            pltpu.VMEM((128, D), F32),
            pltpu.VMEM((3, 1, ROWS), jnp.int32),
            pltpu.VMEM((3, ROWS, 2 * D), BF16),
            pltpu.VMEM((ROWS, 2 * LANES), BF16),
            pltpu.VMEM((ROWS, 2 * LANES), BF16),
            pltpu.VMEM((ROWS, 2 * LANES), BF16),
            pltpu.VMEM((3, 1, ROWS), jnp.int32),
            pltpu.VMEM((DEVS, 3, 4, LANES), jnp.int32),
            pltpu.VMEM((DEVS, 3, 4, LANES), jnp.int32),
            pltpu.VMEM((2, SLOTS, 2 * LANES), BF16),
            pltpu.VMEM((2 * LANES, 3 * D), BF16),
            pltpu.VMEM((N_ROWS * SHARE, 4, LANES), F32),
            pltpu.VMEM((N_ROWS, SHARE, 4, LANES), F32),
            pltpu.VMEM((SHARE, 4, LANES), F32),
            pltpu.VMEM((N_SERVE, SHARE, 4, LANES), F32),
            pltpu.VMEM((N_ROWS, SHARE, 4, LANES), F32),
            pltpu.SemaphoreType.DMA((10,)),
            pltpu.SemaphoreType.DMA,
            pltpu.SemaphoreType.DMA((CHUNKS,)),
            pltpu.SemaphoreType.DMA((3,)),
            pltpu.SemaphoreType.DMA((3,)),
            pltpu.SemaphoreType.DMA,
            pltpu.SemaphoreType.DMA,
        ],
        compiler_params=pltpu.CompilerParams(
            collective_id=0, has_side_effects=True, vmem_limit_bytes=64 << 20
        ),
        cost_estimate=pl.CostEstimate(flops=4_000_000_000, bytes_accessed=8_000_000, transcendentals=0),
        name="step_and_route",
    )(
        rows_small.T, rows_mid.T, rows_wide, row_grads, proj_small, proj_mid, proj_wide,
        counts.T, jnp.transpose(owners, (0, 2, 1)),
    )
    return pl.pallas_call(
        project_kernel,
        grid=(SLOTS // STRIPE,),
        out_shape=jax.ShapeDtypeStruct((SLOTS, 3 * D), BF16),
        in_specs=[
            pl.BlockSpec((2, STRIPE, 2 * LANES), lambda i: (0, i, 0)),
            pl.BlockSpec((2 * LANES, 3 * D), lambda i: (0, 0)),
        ],
        out_specs=pl.BlockSpec((STRIPE, 3 * D), lambda i: (i, 0)),
        compiler_params=pltpu.CompilerParams(vmem_limit_bytes=64 << 20),
        cost_estimate=pl.CostEstimate(flops=1_000_000_000, bytes_accessed=5_000_000, transcendentals=0),
        name="project",
    )(spread, weights)


def solution(mesh):
    return jax.shard_map(
        local,
        mesh=mesh,
        in_specs=(
            P(("rows", "serve"), None),
            P(("rows", "serve"), None),
            P(("rows", "serve"), None),
            P(None, ("rows", "serve"), None),
            P(),
            P(),
            P(),
            P(None, ("rows", "serve")),
            P(None, ("rows", "serve"), None),
        ),
        out_specs=P(("rows", "serve"), None),
        check_vma=False,
    )
```
